32 devices in a mesh: freq: 8 (over y, x, core), slab: 4 (over z).
Axes of the slice: x: 2, y: 2, z: 4, core: 2. Of those that a mesh axis runs over, the one named last changes fastest.
Arguments:
- traces: bfloat16 [98304, 2048], P(('freq', 'slab')), may hold values from -6 to 6
- trace_counts: int32 [32, 8], P(('freq', 'slab')), may hold values from 1 to 512, 3072 in all within a row
- aperture_start: int32 [256], P(('freq', 'slab')), may hold values from 0 to 511
- shot_position: int32 [256], P(('freq', 'slab')), may hold values from 0 to 4095
- rec_slot: int32 [512], replicated, may hold values from 0 to 767, as said below
Outputs:
- encoded: bfloat16 [768, 256, 256], P('slab', 'freq')
The draws below stay inside these ranges and needn't reach their ends.
Inputs may be any that keep to these rules, and one draw needn't show every extreme that they name: `rec_slot`: distinct receivers have distinct slots. No depth slab owns more than 192 receivers, at least one owns exactly 192, and slots 0 and 767 are always used.
All inputs are finite; a program needn't handle non-finite values.
Results may differ from the reference program's by a relative error of at most 0.0062.
Values may be sent and summed in bfloat16 or wider, within the bound.
A program may use at most 192 MiB of HBM per device.

```python
import math
import jax
import jax.numpy as jnp
import numpy as np
from jax import lax

NT = 2048
FREQUENCY_COUNT = 256
F0 = 8
RAY_PARAM_COUNT = 128
NREC = 512
NXS = 4096
RDIV = 16
ROW_DEV = 3072
SHOTS_PER_UNIT = 8
SHOTS = 256
ROWS = 98304
SLAB_SLOT_LIMIT = 192
TOTAL_SLOTS = 768
DEVICES = 32


def draw_rec_slot(key, part):
    owner_of_key, score_of_key, key_order = jax.random.split(key, 3)
    complete_owner_table = jax.random.randint(owner_of_key, (), 0, TOTAL_SLOTS // SLAB_SLOT_LIMIT)
    receiver_slot_index = jnp.arange(TOTAL_SLOTS, dtype=jnp.int32)
    ranking_scores = jax.random.randint(score_of_key, (TOTAL_SLOTS,), 0, 1 << 20) * TOTAL_SLOTS + receiver_slot_index
    pinned_choice = (receiver_slot_index // SLAB_SLOT_LIMIT == complete_owner_table) | (receiver_slot_index == 0) | (receiver_slot_index == TOTAL_SLOTS - 1)
    ranking_scores = jnp.where(pinned_choice, ranking_scores + (1 << 30), ranking_scores)
    unused, chosen = lax.top_k(ranking_scores, NREC)
    shuffle = jax.random.permutation(key_order, NREC)
    return chosen[shuffle].astype(jnp.int32)


def set_ends(array, own_key, low, top_value):
    dims = array.shape
    spot = [jax.random.randint(jax.random.fold_in(own_key, axis), (), 0, dims[axis]) for axis in range(len(dims))]
    array = array.at[tuple(spot)].set(low)
    longest = dims.index(max(dims))
    spot[longest] = (spot[longest] + 1) % dims[longest]
    return array.at[tuple(spot)].set(top_value)


def levels(stream_key, shape, cuts, least, largest):
    loudness = 1.0
    for position, blocks in cuts:
        heights = jax.random.uniform(jax.random.fold_in(jax.random.fold_in(stream_key, 6), position), (blocks,), jnp.float32, least / len(cuts), largest / len(cuts))
        loudness = loudness * jnp.repeat(jnp.exp(heights), shape[position] // blocks).reshape((-1,) + (1,) * (len(shape) - 1 - position))
    return loudness


def profile(count, total, limit, skew):
    loads = [(1 << 20) // math.isqrt(grade ** skew) + 1 for grade in range(2, count + 1)]
    rest, given = total - limit - (count - 1), [1] * (count - 1)
    while rest > 0:
        candidates = [i for i in range(count - 1) if given[i] < limit]
        pool, budget = sum([loads[i] for i in candidates]), rest
        for i in candidates:
            addition = min(limit - given[i], max(1, budget * loads[i] // pool), rest)
            given[i] = given[i] + addition
            rest = rest - addition
    return np.array([limit] + given)


def ragged_sizes(key, amount, total, most, slope):
    if amount == 2:
        one = jax.random.randint(key, (), max(1, total - most), min(most, total - 1) + 1)
        return jnp.stack([one, total - one])
    sizes = jnp.asarray(profile(amount, total, most, slope), jnp.int32)
    pairs = (amount - 1) // 2
    giver, taker = sizes[1:1 + 2 * pairs:2], sizes[2:2 + 2 * pairs:2]
    slack = jnp.minimum(giver - 1, most - taker)
    moved = jax.random.randint(jax.random.fold_in(key, 1), (pairs,), 0, 1 << 20) % (slack + 1)
    sizes = sizes.at[1:1 + 2 * pairs:2].set(giver - moved).at[2:2 + 2 * pairs:2].set(taker + moved)
    return sizes[jax.random.permutation(jax.random.fold_in(key, 2), amount)]


def gaussian(own_key, shape, spread, reach, cuts=(), kind=jnp.bfloat16):
    factor_of = levels(own_key, shape, cuts, -0.22, 0.18) if cuts else 1.0
    array = jax.random.normal(own_key, shape, jnp.float32) * spread * factor_of
    return jnp.minimum(jnp.maximum(array, -reach), reach).astype(kind)


def setup_inputs(seed: int = 0) -> dict:
    streams_of = jax.random.split(jax.random.key(seed), 6)
    return {
        "traces": gaussian(streams_of[0], (ROWS, NT), 1.0, 6.0, ((0, 32),)),
        "trace_counts": jax.vmap(lambda own: ragged_sizes(own, SHOTS_PER_UNIT, ROW_DEV, NREC, 2))(jax.random.split(streams_of[1], DEVICES)).reshape((DEVICES, SHOTS_PER_UNIT)).astype(jnp.int32),
        "aperture_start": set_ends(jax.random.randint(streams_of[2], (SHOTS,), 0, NREC), jax.random.fold_in(streams_of[2], 1), 0, NREC - 1).astype(jnp.int32),
        "shot_position": set_ends(jax.random.randint(streams_of[3], (SHOTS,), 0, NXS), jax.random.fold_in(streams_of[3], 1), 0, NXS - 1).astype(jnp.int32),
        "rec_slot": draw_rec_slot(jax.random.fold_in(streams_of[5], 71), 0),
    }


def dft_factors(freq_bins, samples):
    sample_index = jnp.arange(samples, dtype=jnp.int32)
    phase_index = jnp.remainder(sample_index[:, None] * freq_bins[None, :], samples)
    angle_rad = phase_index.astype(jnp.float32) * (2.0 * math.pi / samples)
    factor = 1.0 / math.sqrt(samples)
    return ((jnp.cos(angle_rad) * factor).astype(jnp.bfloat16), (-jnp.sin(angle_rad) * factor).astype(jnp.bfloat16))

def phase_blocks(freq_bins, positions, total_shots):
    ray_offset = jnp.arange(RAY_PARAM_COUNT, dtype=jnp.int32) - RAY_PARAM_COUNT // 2
    period = NT * RDIV
    product = freq_bins[:, None, None, None] * ray_offset[None, None, None, :] * positions[None, :, :, None]
    angle_rad = jnp.remainder(product, period).astype(jnp.float32) * (2.0 * math.pi / period)
    factor = 1.0 / math.sqrt(total_shots)
    cosine = (jnp.cos(angle_rad) * factor).astype(jnp.bfloat16)
    sine_part = (jnp.sin(angle_rad) * factor).astype(jnp.bfloat16)
    upper_half = jnp.concatenate([cosine, -sine_part], axis=3)
    lower_half = jnp.concatenate([sine_part, cosine], axis=3)
    stacked = jnp.stack([upper_half, lower_half], axis=2)
    return stacked.reshape(freq_bins.shape[0], positions.shape[0] * 2 * positions.shape[1], 2 * RAY_PARAM_COUNT)

def row_layout(counts, starts, row_total, shot_total):
    shot_end = jnp.cumsum(counts).astype(jnp.int32)
    row_index = jnp.arange(row_total, dtype=jnp.int32)
    row_shot = lax.optimization_barrier(jnp.sum((row_index[:, None] >= shot_end[None, :]).astype(jnp.int32), axis=1)).astype(jnp.int32)
    begins = (shot_end - counts).astype(jnp.int32)
    onehot = row_shot[:, None] == jnp.arange(shot_total, dtype=jnp.int32)[None, :]
    row_begin = lax.optimization_barrier(jnp.sum(jnp.where(onehot, begins[None, :], 0), axis=1)).astype(jnp.int32)
    row_start = lax.optimization_barrier(jnp.sum(jnp.where(onehot, starts[None, :], 0), axis=1)).astype(jnp.int32)
    receiver = jnp.remainder(row_start + row_index - row_begin, NREC).astype(jnp.int32)
    return (row_shot, receiver)

def reference(traces, trace_counts, aperture_start, shot_position, rec_slot):
    devices = traces.shape[0] // ROW_DEV
    freq_bins = F0 + jnp.arange(FREQUENCY_COUNT, dtype=jnp.int32)
    cosine_table, sine_table = dft_factors(freq_bins, NT)
    transform = jnp.concatenate([cosine_table, sine_table], axis=1).astype(jnp.float32)
    blocks = traces.reshape(devices, ROW_DEV, NT)
    starts = aperture_start.reshape(devices, SHOTS_PER_UNIT)
    positions = shot_position.reshape(devices, SHOTS_PER_UNIT)

    def one_block(running, inputs):
        block_rows, counts, block_starts, block_positions = inputs
        spectra = jnp.dot(block_rows.astype(jnp.float32), transform, precision=lax.Precision.HIGHEST).astype(jnp.bfloat16)
        row_shot, receiver = row_layout(counts, block_starts, ROW_DEV, SHOTS_PER_UNIT)
        row_slot = rec_slot[receiver]
        filled_lattice = jnp.zeros((TOTAL_SLOTS, FREQUENCY_COUNT, 2 * SHOTS_PER_UNIT), jnp.bfloat16)
        filled_lattice = filled_lattice.at[row_slot, :, row_shot].set(spectra[:, :FREQUENCY_COUNT])
        filled_lattice = filled_lattice.at[row_slot, :, SHOTS_PER_UNIT + row_shot].set(spectra[:, FREQUENCY_COUNT:])
        phases = phase_blocks(freq_bins, block_positions[None, :], SHOTS)
        block_term = jnp.einsum('xfs,fsq->xfq', filled_lattice.astype(jnp.float32), phases.astype(jnp.float32), precision=lax.Precision.HIGHEST)
        return (running + block_term, None)
    initial_value = jnp.zeros((TOTAL_SLOTS, FREQUENCY_COUNT, 2 * RAY_PARAM_COUNT), jnp.float32)
    running, unused = lax.scan(one_block, initial_value, (blocks, trace_counts, starts, positions))
    return running.astype(jnp.bfloat16)
```

```python
import functools
import math

import jax
import jax.numpy as jnp
import ml_dtypes
import numpy as np
from jax import lax
from jax.experimental import pallas as pl
from jax.experimental.pallas import tpu as pltpu
from jax.sharding import PartitionSpec as P

NT = 2048
FREQUENCY_COUNT = 256
F0 = 8
RAY_PARAM_COUNT = 128
NREC = 512
RDIV = 16
LANES = 128
HALF = 64
VMEM_BYTES = 56 * 1024 * 1024


def dft_table(samples):
    bins = F0 + np.arange(FREQUENCY_COUNT, dtype=np.int64)
    index = (bins[:, None] * np.arange(samples, dtype=np.int64)[None, :]) % samples
    angle = index.astype(np.float64) * (2.0 * math.pi / samples)
    factor = 1.0 / math.sqrt(samples)
    table = np.concatenate([np.cos(angle), -np.sin(angle)], axis=0) * factor
    return table.astype(np.float32).astype(ml_dtypes.bfloat16)


def column_slots(slabs, cap):
    whole, rest = cap // LANES, cap % LANES
    assert rest <= HALF
    parts = []
    for slab in range(slabs):
        parts.append(slab * cap + np.arange(whole * LANES))
    for slab in range(slabs if rest else 0):
        lane = np.arange(HALF)
        parts.append(np.where(lane < rest, slab * cap + whole * LANES + lane, -2))
    return np.concatenate(parts).astype(np.int32)


def lattice_kernel(
    slabs, whole, rest, freq_groups, shots, row_steps, window,
    starts, counts, begins, inverse, table, traces, out, spectra, full, part,
):
    step = pl.program_id(0)
    rows = traces.shape[0]
    freq_block = FREQUENCY_COUNT // freq_groups
    pair = freq_block // 2
    block = lax.dot_general(
        table[...], traces[...], (((1,), (1,)), ((), ())), preferred_element_type=jnp.float32
    ).astype(jnp.bfloat16)
    spectra[:, pl.ds(pl.multiple_of(step * rows, rows), rows)] = block

    @pl.when(step == row_steps - 1)
    def _place():
        total = row_steps * rows
        columns = inverse.shape[1]
        full_columns = slabs * whole * LANES
        lane = lax.broadcasted_iota(jnp.int32, (FREQUENCY_COUNT // 2, LANES), 1)

        def one_shot(k, carry):
            begin = begins[k]
            base = pl.multiple_of(
                jnp.minimum((begin // LANES) * LANES, total - window), LANES
            )
            piece = spectra[:, pl.ds(base, window)]
            for first in range(0, columns, 2 * LANES):
                inv = inverse[:, first : first + 2 * LANES]
                offset = jnp.bitwise_and(inv - starts[k], NREC - 1)
                valid = (inv >= 0) & (offset < counts[k])
                target = jnp.where(valid, offset + (begin - base), -1)
                line = lax.broadcasted_iota(jnp.int32, (window, 2 * LANES), 0)
                hot = jnp.where(line == target, 1.0, 0.0).astype(jnp.bfloat16)
                placed = jnp.dot(piece, hot, preferred_element_type=jnp.float32)
                for half in range(2):
                    at = first + half * LANES
                    value = placed[:, half * LANES : (half + 1) * LANES]
                    for c in range(2):
                        mine = value[c * FREQUENCY_COUNT : (c + 1) * FREQUENCY_COUNT]
                        if at < full_columns:
                            full[
                                at // LANES,
                                pl.ds(c * shots + k, FREQUENCY_COUNT, stride=2 * shots),
                                :,
                            ] = mine
                            continue
                        slab = (at - full_columns) // HALF
                        split = mine.reshape(freq_groups, 2, pair, LANES)
                        low = split[:, 0].reshape(freq_groups * pair, LANES)
                        high = split[:, 1].reshape(freq_groups * pair, LANES)
                        spot = pl.ds(c * shots + k, freq_groups * pair, stride=2 * shots)
                        part[slab, spot, :] = jnp.where(lane < HALF, low, pltpu.roll(high, HALF, 1))
                        part[slab + 1, spot, :] = jnp.where(
                            lane < HALF, pltpu.roll(low, HALF, 1), high
                        )
            return carry

        lax.fori_loop(0, shots, one_shot, 0)
        full_rows = freq_block * 2 * shots
        part_rows = pair * 2 * shots

        def deliver(group, carry):
            for slab in range(slabs):
                dest = group * slabs + slab
                for w in range(whole):
                    out[dest, w * full_rows : (w + 1) * full_rows, :] = full[
                        slab * whole + w,
                        pl.ds(pl.multiple_of(group * full_rows, full_rows), full_rows),
                        :,
                    ].astype(jnp.bfloat16)
                if rest:
                    out[dest, whole * full_rows : whole * full_rows + part_rows, :] = part[
                        slab,
                        pl.ds(pl.multiple_of(group * part_rows, part_rows), part_rows),
                        :,
                    ].astype(jnp.bfloat16)
            return carry

        lax.fori_loop(0, freq_groups, deliver, 0)


def make_lattice(traces, counts, starts, rec_slot, slabs, cap, freq_groups):
    row_total, samples = traces.shape
    shots = counts.shape[0]
    whole, rest = cap // LANES, cap % LANES
    rows = 256
    row_steps = row_total // rows
    window = NREC + LANES
    freq_block = FREQUENCY_COUNT // freq_groups
    dest_rows = (whole * freq_block + (freq_block // 2 if rest else 0)) * 2 * shots
    slots = jnp.asarray(column_slots(slabs, cap))
    receivers = jnp.arange(NREC, dtype=jnp.int32)
    inverse = jnp.max(
        jnp.where(rec_slot[:, None] == slots[None, :], receivers[:, None], -1), axis=0
    )[None, :]
    begins = jnp.cumsum(counts) - counts
    smem = pl.BlockSpec(memory_space=pltpu.SMEM)
    return pl.pallas_call(
        functools.partial(
            lattice_kernel, slabs, whole, rest, freq_groups, shots, row_steps, window
        ),
        grid=(row_steps,),
        in_specs=[
            smem,
            smem,
            smem,
            pl.BlockSpec(inverse.shape, lambda i: (0, 0)),
            pl.BlockSpec((2 * FREQUENCY_COUNT, samples), lambda i: (0, 0)),
            pl.BlockSpec((rows, samples), lambda i: (i, 0)),
        ],
        out_specs=pl.BlockSpec((freq_groups * slabs, dest_rows, LANES), lambda i: (0, 0, 0)),
        out_shape=jax.ShapeDtypeStruct(
            (freq_groups * slabs, dest_rows, LANES), jnp.bfloat16
        ),
        scratch_shapes=[
            pltpu.VMEM((2 * FREQUENCY_COUNT, row_total), jnp.bfloat16),
            pltpu.VMEM((max(slabs * whole, 1), FREQUENCY_COUNT * 2 * shots, LANES), jnp.float32),
            pltpu.VMEM((slabs, FREQUENCY_COUNT * shots, LANES), jnp.float32),
        ],
        compiler_params=pltpu.CompilerParams(vmem_limit_bytes=VMEM_BYTES),
        cost_estimate=pl.CostEstimate(
            flops=2 * row_total * samples * 2 * FREQUENCY_COUNT,
            bytes_accessed=row_total * samples * 2,
            transcendentals=0,
        ),
        name="lattice",
    )(starts, counts, begins, inverse, jnp.asarray(dft_table(samples)), traces)


def cos_sin(q, period):
    quarter = period // 4
    shifted = q + quarter // 2
    quadrant = jnp.bitwise_and(shifted // quarter, 3)
    x = (jnp.bitwise_and(shifted, quarter - 1) - quarter // 2).astype(jnp.float32) * (
        2.0 * math.pi / period
    )
    x2 = x * x
    sine = x + x * x2 * (
        -1.6666666666e-1 + x2 * (8.3333333e-3 + x2 * (-1.98412698e-4 + x2 * 2.7557319e-6))
    )
    cosine = 1.0 + x2 * (
        -0.5 + x2 * (4.16666667e-2 + x2 * (-1.38888889e-3 + x2 * 2.48015873e-5))
    )
    swap = jnp.bitwise_and(quadrant, 1) == 1
    c = jnp.where(swap, sine, cosine)
    s = jnp.where(swap, cosine, sine)
    c = jnp.where((quadrant == 1) | (quadrant == 2), -c, c)
    s = jnp.where(quadrant >= 2, -s, s)
    return c, s


def phase_kernel(shots, total_shots, first_bin, positions, out):
    bin_index = first_bin[0] + pl.program_id(0)
    rays = lax.broadcasted_iota(jnp.int32, positions.shape, 1) - RAY_PARAM_COUNT // 2
    period = NT * RDIV
    q = jnp.bitwise_and(bin_index * rays * positions[...], period - 1)
    c, s = cos_sin(q, period)
    factor = 1.0 / math.sqrt(total_shots)
    sources = positions.shape[0] // shots
    c = (c * factor).reshape(sources, 1, shots, RAY_PARAM_COUNT)
    s = (s * factor).reshape(sources, 1, shots, RAY_PARAM_COUNT)
    left = jnp.concatenate([c, s], axis=1).reshape(sources * 2 * shots, RAY_PARAM_COUNT)
    right = jnp.concatenate([-s, c], axis=1).reshape(sources * 2 * shots, RAY_PARAM_COUNT)
    out[0, :, :RAY_PARAM_COUNT] = left.astype(jnp.bfloat16)
    out[0, :, RAY_PARAM_COUNT:] = right.astype(jnp.bfloat16)


def make_phases(positions, first_bin, freq_block, shots):
    total_shots = positions.shape[0]
    wide = jnp.broadcast_to(positions[:, None], (total_shots, RAY_PARAM_COUNT))
    return pl.pallas_call(
        functools.partial(phase_kernel, shots, total_shots),
        grid=(freq_block,),
        in_specs=[
            pl.BlockSpec(memory_space=pltpu.SMEM),
            pl.BlockSpec((total_shots, RAY_PARAM_COUNT), lambda i: (0, 0)),
        ],
        out_specs=pl.BlockSpec((1, 2 * total_shots, 2 * RAY_PARAM_COUNT), lambda i: (i, 0, 0)),
        out_shape=jax.ShapeDtypeStruct(
            (freq_block, 2 * total_shots, 2 * RAY_PARAM_COUNT), jnp.bfloat16
        ),
        compiler_params=pltpu.CompilerParams(vmem_limit_bytes=VMEM_BYTES),
        cost_estimate=pl.CostEstimate(
            flops=freq_block * total_shots * RAY_PARAM_COUNT * 40,
            bytes_accessed=freq_block * total_shots * 8 * RAY_PARAM_COUNT,
            transcendentals=0,
        ),
        name="phases",
    )(first_bin, wide)


def encode_kernel(cap, whole, rest, pair, *refs):
    blocks = refs[: 2 * whole + (1 if rest else 0)]
    low_phase, high_phase, out, summed = refs[len(blocks) :]
    step = pl.program_id(0)
    freq_block = 2 * pair
    depth = low_phase.shape[1]
    over_rows = (((0,), (0,)), ((), ()))

    def put(slot, f, value):
        spot = pl.ds(slot * freq_block + f, value.shape[0], stride=freq_block)
        for half in range(2):
            summed[half, spot, :] = value[:, half * LANES : (half + 1) * LANES]

    for w in range(whole):
        for side, phase in enumerate((low_phase, high_phase)):
            held = blocks[2 * w + side][...].reshape(depth, LANES)
            value = lax.dot_general(
                held, phase[0], over_rows, preferred_element_type=jnp.float32
            )
            put(w * LANES, step + side * pair, value)
    if rest:
        held = blocks[2 * whole][...].reshape(depth, LANES)
        for side, phase in enumerate((low_phase, high_phase)):
            value = lax.dot_general(
                held, phase[0], over_rows, preferred_element_type=jnp.float32
            )
            put(whole * LANES, step + side * pair, value[side * HALF : side * HALF + rest])

    @pl.when(step == pair - 1)
    def _round():
        chunk = 16

        def one(i, carry):
            for half in range(2):
                value = summed[
                    half, pl.ds(pl.multiple_of(i * chunk * freq_block, 8), chunk * freq_block), :
                ]
                out[pl.ds(i * chunk, chunk), :, half * LANES : (half + 1) * LANES] = value.reshape(
                    chunk, freq_block, LANES
                ).astype(jnp.bfloat16)
            return carry

        lax.fori_loop(0, cap // chunk, one, 0)


def encode(received, phases, cap, freq_block, shots):
    sources = received.shape[0]
    whole, rest = cap // LANES, cap % LANES
    pair = freq_block // 2
    group = 2 * shots
    held = received.reshape(sources, -1, group, LANES)

    def spec(first):
        return pl.BlockSpec((sources, 1, group, LANES), lambda i: (0, first + i, 0, 0))

    firsts = []
    for w in range(whole):
        firsts += [w * freq_block, w * freq_block + pair]
    if rest:
        firsts.append(whole * freq_block)
    depth = phases.shape[1]
    return pl.pallas_call(
        functools.partial(encode_kernel, cap, whole, rest, pair),
        grid=(pair,),
        in_specs=[spec(first) for first in firsts]
        + [
            pl.BlockSpec((1, depth, 2 * RAY_PARAM_COUNT), lambda i: (i, 0, 0)),
            pl.BlockSpec((1, depth, 2 * RAY_PARAM_COUNT), lambda i: (i + pair, 0, 0)),
        ],
        out_specs=pl.BlockSpec((cap, freq_block, 2 * RAY_PARAM_COUNT), lambda i: (0, 0, 0)),
        out_shape=jax.ShapeDtypeStruct((cap, freq_block, 2 * RAY_PARAM_COUNT), jnp.bfloat16),
        scratch_shapes=[pltpu.VMEM((2, cap * freq_block, LANES), jnp.float32)],
        compiler_params=pltpu.CompilerParams(vmem_limit_bytes=VMEM_BYTES),
        name="encode",
    )(*([held] * len(firsts)), phases, phases)


def on_device(traces, trace_counts, aperture_start, shot_position, rec_slot):
    shots = trace_counts.shape[1]
    freq_groups = lax.axis_size("freq")
    slabs = lax.axis_size("slab")
    freq_block = FREQUENCY_COUNT // freq_groups
    cap = 3 * NREC // (2 * slabs)
    axes = ("freq", "slab")
    positions = lax.all_gather(shot_position, axes, axis=0, tiled=True)
    lattice = make_lattice(
        traces, trace_counts[0], aperture_start, rec_slot, slabs, cap, freq_groups
    )
    received = lax.all_to_all(lattice, axes, split_axis=0, concat_axis=0, tiled=True)
    first_bin = (F0 + lax.axis_index("freq") * freq_block).astype(jnp.int32)[None]
    phases = make_phases(positions, first_bin, freq_block, shots)
    return encode(received, phases, cap, freq_block, shots)


def solution(mesh):
    return jax.shard_map(
        on_device,
        mesh=mesh,
        in_specs=(
            P(("freq", "slab"), None),
            P(("freq", "slab"), None),
            P(("freq", "slab")),
            P(("freq", "slab")),
            P(),
        ),
        out_specs=P("slab", "freq", None),
        check_vma=False,
    )
```

```python
import functools
import math

import jax
import jax.numpy as jnp
import ml_dtypes
import numpy as np
from jax import lax
from jax.experimental import pallas as pl
from jax.experimental.pallas import tpu as pltpu
from jax.sharding import PartitionSpec as P

NT = 2048
FREQUENCY_COUNT = 256
F0 = 8
RAY_PARAM_COUNT = 128
NREC = 512
RDIV = 16
LANES = 128
HALF = 64
VMEM_BYTES = 56 * 1024 * 1024


def dft_table(samples):
    bins = F0 + np.arange(FREQUENCY_COUNT, dtype=np.int64)
    index = (bins[:, None] * np.arange(samples, dtype=np.int64)[None, :]) % samples
    angle = index.astype(np.float64) * (2.0 * math.pi / samples)
    factor = 1.0 / math.sqrt(samples)
    table = np.concatenate([np.cos(angle), -np.sin(angle)], axis=0) * factor
    return table.astype(np.float32).astype(ml_dtypes.bfloat16)


def chunk_columns(slabs, cap, chunk):
    lane = chunk * HALF + np.arange(HALF)
    slots = [np.where(lane < cap, slab * cap + lane, -2) for slab in range(slabs)]
    return np.concatenate(slots).astype(np.int32)


def place(slabs, freq_groups, shots, starts, counts, inverse, spectra, out, part):
    total = spectra.shape[1]
    window = NREC + LANES
    pair = FREQUENCY_COUNT // freq_groups // 2
    lane = lax.broadcasted_iota(jnp.int32, (FREQUENCY_COUNT // 2, LANES), 1)

    def one_shot(k, begin):
        base = pl.multiple_of(jnp.minimum((begin // LANES) * LANES, total - window), LANES)
        piece = spectra[:, pl.ds(base, window)]
        for first in range(0, slabs * HALF, 2 * LANES):
            inv = inverse[:, first : first + 2 * LANES]
            offset = jnp.bitwise_and(inv - starts[k], NREC - 1)
            valid = (inv >= 0) & (offset < counts[k])
            target = jnp.where(valid, offset + (begin - base), -1)
            line = lax.broadcasted_iota(jnp.int32, (window, 2 * LANES), 0)
            hot = jnp.where(line == target, 1.0, 0.0).astype(jnp.bfloat16)
            placed = jnp.dot(piece, hot, preferred_element_type=jnp.float32)
            for half in range(2):
                slab = (first + half * LANES) // HALF
                value = placed[:, half * LANES : (half + 1) * LANES]
                for c in range(2):
                    mine = value[c * FREQUENCY_COUNT : (c + 1) * FREQUENCY_COUNT]
                    split = mine.reshape(freq_groups, 2, pair, LANES)
                    low = split[:, 0].reshape(freq_groups * pair, LANES)
                    high = split[:, 1].reshape(freq_groups * pair, LANES)
                    spot = pl.ds(c * shots + k, freq_groups * pair, stride=2 * shots)
                    part[slab, spot, :] = jnp.where(lane < HALF, low, pltpu.roll(high, HALF, 1))
                    part[slab + 1, spot, :] = jnp.where(lane < HALF, pltpu.roll(low, HALF, 1), high)
        return begin + counts[k]

    lax.fori_loop(0, shots, one_shot, 0)
    rows = pair * 2 * shots

    def deliver(group, carry):
        for slab in range(slabs):
            out[group * slabs + slab, :rows, :] = part[
                slab, pl.ds(pl.multiple_of(group * rows, rows), rows), :
            ].astype(jnp.bfloat16)
        return carry

    lax.fori_loop(0, freq_groups, deliver, 0)


def first_kernel(
    slabs, freq_groups, shots, row_steps,
    starts, counts, positions, inverse, table, traces, spectra, out, part,
):
    step = pl.program_id(0)
    rows = traces.shape[0]
    block = lax.dot_general(
        table[...], traces[...], (((1,), (1,)), ((), ())), preferred_element_type=jnp.float32
    ).astype(jnp.bfloat16)
    spectra[:, pl.ds(pl.multiple_of(step * rows, rows), rows)] = block

    @pl.when(step == row_steps - 1)
    def _place():
        place(slabs, freq_groups, shots, starts, counts, inverse, spectra, out, part)
        line = lax.broadcasted_iota(jnp.int32, (2 * shots, LANES), 0)
        halves = jnp.zeros((2 * shots, LANES), jnp.int32)
        for k in range(shots):
            halves = jnp.where(line == k, positions[k] // HALF, halves)
            halves = jnp.where(line == shots + k, positions[k] % HALF, halves)
        coded = halves.astype(jnp.float32).astype(jnp.bfloat16)
        rows_used = out.shape[1] - 2 * shots
        for dest in range(out.shape[0]):
            out[dest, rows_used:, :] = coded


def later_kernel(slabs, freq_groups, shots, starts, counts, inverse, spectra, out, part):
    place(slabs, freq_groups, shots, starts, counts, inverse, spectra, out, part)


def chunk_inverse(rec_slot, slabs, cap, chunk):
    slots = jnp.asarray(chunk_columns(slabs, cap, chunk))
    receivers = jnp.arange(NREC, dtype=jnp.int32)
    return jnp.max(
        jnp.where(rec_slot[:, None] == slots[None, :], receivers[:, None], -1), axis=0
    )[None, :]


def part_shape(slabs, shots):
    return pltpu.VMEM((slabs, FREQUENCY_COUNT * shots, LANES), jnp.float32)


def first_chunk(traces, counts, starts, positions, inverse, slabs, freq_groups):
    row_total, samples = traces.shape
    shots = counts.shape[0]
    rows = 256
    row_steps = row_total // rows
    dests = freq_groups * slabs
    dest_rows = (FREQUENCY_COUNT // freq_groups // 2 + 1) * 2 * shots
    smem = pl.BlockSpec(memory_space=pltpu.SMEM)
    return pl.pallas_call(
        functools.partial(first_kernel, slabs, freq_groups, shots, row_steps),
        grid=(row_steps,),
        in_specs=[
            smem,
            smem,
            smem,
            pl.BlockSpec(inverse.shape, lambda i: (0, 0)),
            pl.BlockSpec((2 * FREQUENCY_COUNT, samples), lambda i: (0, 0)),
            pl.BlockSpec((rows, samples), lambda i: (i, 0)),
        ],
        out_specs=[
            pl.BlockSpec((2 * FREQUENCY_COUNT, row_total), lambda i: (0, 0)),
            pl.BlockSpec((dests, dest_rows, LANES), lambda i: (0, 0, 0)),
        ],
        out_shape=[
            jax.ShapeDtypeStruct((2 * FREQUENCY_COUNT, row_total), jnp.bfloat16),
            jax.ShapeDtypeStruct((dests, dest_rows, LANES), jnp.bfloat16),
        ],
        scratch_shapes=[part_shape(slabs, shots)],
        compiler_params=pltpu.CompilerParams(vmem_limit_bytes=VMEM_BYTES),
        cost_estimate=pl.CostEstimate(
            flops=2 * row_total * samples * 2 * FREQUENCY_COUNT,
            bytes_accessed=row_total * samples * 2,
            transcendentals=0,
        ),
        name="first_chunk",
    )(starts, counts, positions, inverse, jnp.asarray(dft_table(samples)), traces)


def later_chunk(spectra, counts, starts, inverse, slabs, freq_groups):
    shots = counts.shape[0]
    dests = freq_groups * slabs
    dest_rows = FREQUENCY_COUNT // freq_groups // 2 * 2 * shots
    smem = pl.BlockSpec(memory_space=pltpu.SMEM)
    vmem = pl.BlockSpec(memory_space=pltpu.VMEM)
    return pl.pallas_call(
        functools.partial(later_kernel, slabs, freq_groups, shots),
        in_specs=[smem, smem, vmem, vmem],
        out_specs=vmem,
        out_shape=jax.ShapeDtypeStruct((dests, dest_rows, LANES), jnp.bfloat16),
        scratch_shapes=[part_shape(slabs, shots)],
        compiler_params=pltpu.CompilerParams(vmem_limit_bytes=VMEM_BYTES),
        cost_estimate=pl.CostEstimate(
            flops=2 * 2 * FREQUENCY_COUNT * shots * 640 * slabs * HALF,
            bytes_accessed=12 * 1024 * 1024,
            transcendentals=0,
        ),
        name="later_chunk",
    )(starts, counts, inverse, spectra)


def cos_sin(q, period):
    quarter = period // 4
    shifted = q + quarter // 2
    quadrant = jnp.bitwise_and(shifted // quarter, 3)
    x = (jnp.bitwise_and(shifted, quarter - 1) - quarter // 2).astype(jnp.float32) * (
        2.0 * math.pi / period
    )
    x2 = x * x
    sine = x + x * x2 * (
        -1.6666666666e-1 + x2 * (8.3333333e-3 + x2 * (-1.98412698e-4 + x2 * 2.7557319e-6))
    )
    cosine = 1.0 + x2 * (
        -0.5 + x2 * (4.16666667e-2 + x2 * (-1.38888889e-3 + x2 * 2.48015873e-5))
    )
    swap = jnp.bitwise_and(quadrant, 1) == 1
    c = jnp.where(swap, sine, cosine)
    s = jnp.where(swap, cosine, sine)
    c = jnp.where((quadrant == 1) | (quadrant == 2), -c, c)
    s = jnp.where(quadrant >= 2, -s, s)
    return c, s


def phase_kernel(shots, total_shots, first_bin, halves, out):
    bin_index = first_bin[0] + pl.program_id(0)
    sources = halves.shape[0]
    coded = halves[...].reshape(sources, 2 * shots, LANES).astype(jnp.float32)
    positions = (coded[:, :shots] * HALF + coded[:, shots:]).astype(jnp.int32)
    rays = lax.broadcasted_iota(jnp.int32, positions.shape, 2) - RAY_PARAM_COUNT // 2
    period = NT * RDIV
    q = jnp.bitwise_and(bin_index * rays * positions, period - 1)
    c, s = cos_sin(q, period)
    factor = 1.0 / math.sqrt(total_shots)
    c = (c * factor)[:, None]
    s = (s * factor)[:, None]
    left = jnp.concatenate([c, s], axis=1).reshape(sources * 2 * shots, RAY_PARAM_COUNT)
    right = jnp.concatenate([-s, c], axis=1).reshape(sources * 2 * shots, RAY_PARAM_COUNT)
    out[0, :, :RAY_PARAM_COUNT] = left.astype(jnp.bfloat16)
    out[0, :, RAY_PARAM_COUNT:] = right.astype(jnp.bfloat16)


def make_phases(received, first_bin, freq_block, shots):
    sources = received.shape[0]
    total_shots = sources * shots
    held = received.reshape(sources, -1, 2 * shots, LANES)
    last = held.shape[1] - 1
    return pl.pallas_call(
        functools.partial(phase_kernel, shots, total_shots),
        grid=(freq_block,),
        in_specs=[
            pl.BlockSpec(memory_space=pltpu.SMEM),
            pl.BlockSpec((sources, 1, 2 * shots, LANES), lambda i: (0, last, 0, 0)),
        ],
        out_specs=pl.BlockSpec((1, 2 * total_shots, 2 * RAY_PARAM_COUNT), lambda i: (i, 0, 0)),
        out_shape=jax.ShapeDtypeStruct(
            (freq_block, 2 * total_shots, 2 * RAY_PARAM_COUNT), jnp.bfloat16
        ),
        compiler_params=pltpu.CompilerParams(vmem_limit_bytes=VMEM_BYTES),
        cost_estimate=pl.CostEstimate(
            flops=freq_block * total_shots * RAY_PARAM_COUNT * 40,
            bytes_accessed=64 * 1024 * 1024,
            transcendentals=0,
        ),
        name="phases",
    )(first_bin, held)


def encode_kernel(slots, pair, *refs):
    held, low_phase, high_phase = refs[:3]
    out, summed = refs[-2:]
    step = pl.program_id(0)
    freq_block = 2 * pair
    depth = low_phase.shape[1]
    columns = held[...].reshape(depth, LANES)
    for side, phase in enumerate((low_phase, high_phase)):
        value = lax.dot_general(
            columns, phase[0], (((0,), (0,)), ((), ())), preferred_element_type=jnp.float32
        )[side * HALF : side * HALF + slots]
        spot = pl.ds(step + side * pair, slots, stride=freq_block)
        for half in range(2):
            summed[half, spot, :] = value[:, half * LANES : (half + 1) * LANES]

    @pl.when(step == pair - 1)
    def _round():
        chunk = 16

        def one(i, carry):
            for half in range(2):
                value = summed[
                    half, pl.ds(pl.multiple_of(i * chunk * freq_block, 8), chunk * freq_block), :
                ]
                out[pl.ds(i * chunk, chunk), :, half * LANES : (half + 1) * LANES] = value.reshape(
                    chunk, freq_block, LANES
                ).astype(jnp.bfloat16)
            return carry

        lax.fori_loop(0, slots // chunk, one, 0)


def encode(received, phases, before, chunk, cap, freq_block, shots):
    sources = received.shape[0]
    pair = freq_block // 2
    group = 2 * shots
    held = received.reshape(sources, -1, group, LANES)
    slots = min(cap, HALF)
    depth = phases.shape[1]
    in_specs = [
        pl.BlockSpec((sources, 1, group, LANES), lambda i: (0, i, 0, 0)),
        pl.BlockSpec((1, depth, 2 * RAY_PARAM_COUNT), lambda i: (i, 0, 0)),
        pl.BlockSpec((1, depth, 2 * RAY_PARAM_COUNT), lambda i: (i + pair, 0, 0)),
    ]
    operands = [held, phases, phases]
    aliases = {}
    if before is not None:
        in_specs.append(pl.BlockSpec(memory_space=pl.ANY))
        operands.append(before)
        aliases = {3: 0}
    return pl.pallas_call(
        functools.partial(encode_kernel, slots, pair),
        grid=(pair,),
        in_specs=in_specs,
        out_specs=pl.BlockSpec((slots, freq_block, 2 * RAY_PARAM_COUNT), lambda i: (chunk, 0, 0)),
        out_shape=jax.ShapeDtypeStruct((cap, freq_block, 2 * RAY_PARAM_COUNT), jnp.bfloat16),
        scratch_shapes=[pltpu.VMEM((2, slots * freq_block, LANES), jnp.float32)],
        input_output_aliases=aliases,
        compiler_params=pltpu.CompilerParams(vmem_limit_bytes=VMEM_BYTES),
        cost_estimate=pl.CostEstimate(
            flops=2 * freq_block * depth * LANES * 2 * RAY_PARAM_COUNT,
            bytes_accessed=24 * 1024 * 1024,
            transcendentals=0,
        ),
        name="encode",
    )(*operands)


def on_device(traces, trace_counts, aperture_start, shot_position, rec_slot):
    shots = trace_counts.shape[1]
    freq_groups = lax.axis_size("freq")
    slabs = lax.axis_size("slab")
    freq_block = FREQUENCY_COUNT // freq_groups
    cap = 3 * NREC // (2 * slabs)
    chunks = -(-cap // HALF)
    assert cap % min(cap, HALF) == 0
    counts = trace_counts[0]
    inverses = [chunk_inverse(rec_slot, slabs, cap, chunk) for chunk in range(chunks)]
    spectra, first_sent = first_chunk(
        traces, counts, aperture_start, shot_position, inverses[0], slabs, freq_groups
    )
    sent = [first_sent] + [
        later_chunk(spectra, counts, aperture_start, inverse, slabs, freq_groups)
        for inverse in inverses[1:]
    ]
    first_bin = (F0 + lax.axis_index("freq") * freq_block).astype(jnp.int32)[None]
    encoded, phases = None, None
    received = exchange(sent[0])
    for chunk in range(chunks):
        upcoming = None
        if chunk + 1 < chunks:
            held = (received, sent[chunk + 1 :]) + (() if encoded is None else (encoded,))
            held = lax.optimization_barrier(held)
            received, sent[chunk + 1 :] = held[0], held[1]
            encoded = held[2] if encoded is not None else None
            upcoming = exchange(sent[chunk + 1])
        if chunk == 0:
            phases = make_phases(received, first_bin, freq_block, shots)
        encoded = encode(received, phases, encoded, chunk, cap, freq_block, shots)
        received = upcoming
    return encoded


def exchange(sent):
    return lax.all_to_all(sent, ("freq", "slab"), split_axis=0, concat_axis=0, tiled=True)


def solution(mesh):
    return jax.shard_map(
        on_device,
        mesh=mesh,
        in_specs=(
            P(("freq", "slab"), None),
            P(("freq", "slab"), None),
            P(("freq", "slab")),
            P(("freq", "slab")),
            P(),
        ),
        out_specs=P("slab", "freq", None),
        check_vma=False,
    )
```

```python
import functools
import math

import jax
import jax.numpy as jnp
import ml_dtypes
import numpy as np
from jax import lax
from jax.experimental import pallas as pl
from jax.experimental.pallas import tpu as pltpu
from jax.sharding import PartitionSpec as P

NT = 2048
FREQUENCY_COUNT = 256
F0 = 8
RAY_PARAM_COUNT = 128
NREC = 512
RDIV = 16
LANES = 128
HALF = 64
HALVES = 2
BINS = FREQUENCY_COUNT // HALVES
VMEM_BYTES = 56 * 1024 * 1024


def dft_table(samples, freq_groups, half):
    share = FREQUENCY_COUNT // freq_groups // HALVES
    owners = np.arange(freq_groups, dtype=np.int64)[:, None] * (HALVES * share)
    bins = (F0 + owners + half * share + np.arange(share, dtype=np.int64)[None, :]).reshape(-1)
    index = (np.arange(samples, dtype=np.int64)[:, None] * bins[None, :]) % samples
    angle = index.astype(np.float64) * (2.0 * math.pi / samples)
    factor = 1.0 / math.sqrt(samples)
    table = np.concatenate([np.cos(angle), -np.sin(angle)], axis=1) * factor
    return table.astype(np.float32).astype(ml_dtypes.bfloat16)


def chunk_columns(slabs, cap, chunk):
    lane = chunk * HALF + np.arange(HALF)
    slots = [np.where(lane < cap, slab * cap + lane, -2) for slab in range(slabs)]
    return np.concatenate(slots).astype(np.int32)


def place(slabs, freq_groups, shots, starts, counts, inverse, spectra, out, part):
    total = spectra.shape[1]
    window = NREC + LANES
    pair = BINS // freq_groups // 2
    lane = lax.broadcasted_iota(jnp.int32, (BINS // 2, LANES), 1)

    def one_shot(k, begin):
        base = pl.multiple_of(jnp.minimum((begin // LANES) * LANES, total - window), LANES)
        piece = spectra[:, pl.ds(base, window)]
        for first in range(0, slabs * HALF, 2 * LANES):
            inv = inverse[:, first : first + 2 * LANES]
            offset = jnp.bitwise_and(inv - starts[k], NREC - 1)
            valid = (inv >= 0) & (offset < counts[k])
            target = jnp.where(valid, offset + (begin - base), -1)
            line = lax.broadcasted_iota(jnp.int32, (window, 2 * LANES), 0)
            hot = jnp.where(line == target, 1.0, 0.0).astype(jnp.bfloat16)
            placed = jnp.dot(piece, hot, preferred_element_type=jnp.float32)
            for half in range(2):
                slab = (first + half * LANES) // HALF
                value = placed[:, half * LANES : (half + 1) * LANES]
                for c in range(2):
                    mine = value[c * BINS : (c + 1) * BINS]
                    split = mine.reshape(freq_groups, 2, pair, LANES)
                    low = split[:, 0].reshape(freq_groups * pair, LANES)
                    high = split[:, 1].reshape(freq_groups * pair, LANES)
                    spot = pl.ds(c * shots + k, freq_groups * pair, stride=2 * shots)
                    part[slab, spot, :] = jnp.where(lane < HALF, low, pltpu.roll(high, HALF, 1))
                    part[slab + 1, spot, :] = jnp.where(lane < HALF, pltpu.roll(low, HALF, 1), high)
        return begin + counts[k]

    lax.fori_loop(0, shots, one_shot, 0)
    rows = pair * 2 * shots

    def deliver(group, carry):
        for slab in range(slabs):
            out[group * slabs + slab, :rows, :] = part[
                slab, pl.ds(pl.multiple_of(group * rows, rows), rows), :
            ].astype(jnp.bfloat16)
        return carry

    lax.fori_loop(0, freq_groups, deliver, 0)


def first_kernel(
    slabs, freq_groups, shots, row_steps, with_positions,
    starts, counts, positions, inverse, table, traces, spectra, out, part,
):
    step = pl.program_id(0)
    rows = traces.shape[0]
    block = jnp.dot(traces[...], table[...], preferred_element_type=jnp.float32)
    spectra[:, pl.ds(pl.multiple_of(step * rows, rows), rows)] = block.T.astype(jnp.bfloat16)

    @pl.when(step == row_steps - 1)
    def _place():
        place(slabs, freq_groups, shots, starts, counts, inverse, spectra, out, part)
        if not with_positions:
            return
        line = lax.broadcasted_iota(jnp.int32, (2 * shots, LANES), 0)
        halves = jnp.zeros((2 * shots, LANES), jnp.int32)
        for k in range(shots):
            halves = jnp.where(line == k, positions[k] // HALF, halves)
            halves = jnp.where(line == shots + k, positions[k] % HALF, halves)
        coded = halves.astype(jnp.float32).astype(jnp.bfloat16)
        rows_used = out.shape[1] - 2 * shots
        for dest in range(out.shape[0]):
            out[dest, rows_used:, :] = coded


def later_kernel(slabs, freq_groups, shots, starts, counts, inverse, spectra, out, part):
    place(slabs, freq_groups, shots, starts, counts, inverse, spectra, out, part)


def chunk_inverse(rec_slot, slabs, cap, chunk):
    slots = jnp.asarray(chunk_columns(slabs, cap, chunk))
    receivers = jnp.arange(NREC, dtype=jnp.int32)
    return jnp.max(
        jnp.where(rec_slot[:, None] == slots[None, :], receivers[:, None], -1), axis=0
    )[None, :]


def part_shape(slabs, shots):
    return pltpu.VMEM((slabs, BINS * shots, LANES), jnp.float32)


def first_chunk(traces, counts, starts, positions, inverse, slabs, freq_groups, half):
    row_total, samples = traces.shape
    shots = counts.shape[0]
    rows = 512
    row_steps = row_total // rows
    dests = freq_groups * slabs
    with_positions = half == 0
    dest_rows = (BINS // freq_groups // 2 + (1 if with_positions else 0)) * 2 * shots
    smem = pl.BlockSpec(memory_space=pltpu.SMEM)
    return pl.pallas_call(
        functools.partial(first_kernel, slabs, freq_groups, shots, row_steps, with_positions),
        grid=(row_steps,),
        in_specs=[
            smem,
            smem,
            smem,
            pl.BlockSpec(inverse.shape, lambda i: (0, 0)),
            pl.BlockSpec((samples, 2 * BINS), lambda i: (0, 0)),
            pl.BlockSpec((rows, samples), lambda i: (i, 0)),
        ],
        out_specs=[
            pl.BlockSpec((2 * BINS, row_total), lambda i: (0, 0)),
            pl.BlockSpec((dests, dest_rows, LANES), lambda i: (0, 0, 0)),
        ],
        out_shape=[
            jax.ShapeDtypeStruct((2 * BINS, row_total), jnp.bfloat16),
            jax.ShapeDtypeStruct((dests, dest_rows, LANES), jnp.bfloat16),
        ],
        scratch_shapes=[part_shape(slabs, shots)],
        compiler_params=pltpu.CompilerParams(vmem_limit_bytes=VMEM_BYTES),
        cost_estimate=pl.CostEstimate(
            flops=2 * row_total * samples * 2 * BINS,
            bytes_accessed=row_total * samples * 2,
            transcendentals=0,
        ),
        name="first_chunk",
    )(
        starts, counts, positions, inverse,
        jnp.asarray(dft_table(samples, freq_groups, half)), traces,
    )


def later_chunk(spectra, counts, starts, inverse, slabs, freq_groups):
    shots = counts.shape[0]
    dests = freq_groups * slabs
    dest_rows = BINS // freq_groups // 2 * 2 * shots
    smem = pl.BlockSpec(memory_space=pltpu.SMEM)
    vmem = pl.BlockSpec(memory_space=pltpu.VMEM)
    return pl.pallas_call(
        functools.partial(later_kernel, slabs, freq_groups, shots),
        in_specs=[smem, smem, vmem, vmem],
        out_specs=vmem,
        out_shape=jax.ShapeDtypeStruct((dests, dest_rows, LANES), jnp.bfloat16),
        scratch_shapes=[part_shape(slabs, shots)],
        compiler_params=pltpu.CompilerParams(vmem_limit_bytes=VMEM_BYTES),
        cost_estimate=pl.CostEstimate(
            flops=2 * 2 * BINS * shots * 640 * slabs * HALF,
            bytes_accessed=6 * 1024 * 1024,
            transcendentals=0,
        ),
        name="later_chunk",
    )(starts, counts, inverse, spectra)


def cos_sin(q, period):
    quarter = period // 4
    shifted = q + quarter // 2
    quadrant = jnp.bitwise_and(shifted // quarter, 3)
    x = (jnp.bitwise_and(shifted, quarter - 1) - quarter // 2).astype(jnp.float32) * (
        2.0 * math.pi / period
    )
    x2 = x * x
    sine = x + x * x2 * (
        -1.6666666666e-1 + x2 * (8.3333333e-3 + x2 * (-1.98412698e-4 + x2 * 2.7557319e-6))
    )
    cosine = 1.0 + x2 * (
        -0.5 + x2 * (4.16666667e-2 + x2 * (-1.38888889e-3 + x2 * 2.48015873e-5))
    )
    swap = jnp.bitwise_and(quadrant, 1) == 1
    c = jnp.where(swap, sine, cosine)
    s = jnp.where(swap, cosine, sine)
    c = jnp.where((quadrant == 1) | (quadrant == 2), -c, c)
    s = jnp.where(quadrant >= 2, -s, s)
    return c, s


def phase_kernel(shots, total_shots, pair, first_bin, halves, out):
    sources = halves.shape[0]
    coded = halves[...].reshape(sources, 2 * shots, LANES).astype(jnp.float32)
    positions = (coded[:, :shots] * HALF + coded[:, shots:]).astype(jnp.int32)
    rays = lax.broadcasted_iota(jnp.int32, positions.shape, 2) - RAY_PARAM_COUNT // 2
    period = NT * RDIV
    factor = 1.0 / math.sqrt(total_shots)
    for side in range(2):
        bin_index = first_bin[0] + pl.program_id(0) + side * pair
        q = jnp.bitwise_and(bin_index * rays * positions, period - 1)
        c, s = cos_sin(q, period)
        c = (c * factor)[:, None]
        s = (s * factor)[:, None]
        left = jnp.concatenate([c, s], axis=1).reshape(sources * 2 * shots, RAY_PARAM_COUNT)
        right = jnp.concatenate([-s, c], axis=1).reshape(sources * 2 * shots, RAY_PARAM_COUNT)
        at = 2 * side * RAY_PARAM_COUNT
        out[0, :, at : at + RAY_PARAM_COUNT] = left.astype(jnp.bfloat16)
        out[0, :, at + RAY_PARAM_COUNT : at + 2 * RAY_PARAM_COUNT] = right.astype(jnp.bfloat16)


def make_phases(received, first_bin, pair, shots):
    sources = received.shape[0]
    total_shots = sources * shots
    held = received.reshape(sources, -1, 2 * shots, LANES)
    last = held.shape[1] - 1
    return pl.pallas_call(
        functools.partial(phase_kernel, shots, total_shots, pair),
        grid=(pair,),
        in_specs=[
            pl.BlockSpec(memory_space=pltpu.SMEM),
            pl.BlockSpec((sources, 1, 2 * shots, LANES), lambda i: (0, last, 0, 0)),
        ],
        out_specs=pl.BlockSpec((1, 2 * total_shots, 4 * RAY_PARAM_COUNT), lambda i: (i, 0, 0)),
        out_shape=jax.ShapeDtypeStruct(
            (pair, 2 * total_shots, 4 * RAY_PARAM_COUNT), jnp.bfloat16
        ),
        compiler_params=pltpu.CompilerParams(vmem_limit_bytes=VMEM_BYTES),
        cost_estimate=pl.CostEstimate(
            flops=pair * total_shots * RAY_PARAM_COUNT * 80,
            bytes_accessed=32 * 1024 * 1024,
            transcendentals=0,
        ),
        name="phases",
    )(first_bin, held)


def encode_kernel(slots, pair, each, *refs):
    held, phases = refs[:2]
    out, summed = refs[-2:]
    step = pl.program_id(0)
    share = 2 * pair
    depth = phases.shape[1]
    width = 2 * RAY_PARAM_COUNT
    for item in range(each):
        value = lax.dot_general(
            held[:, item].reshape(depth, LANES),
            phases[item],
            (((0,), (0,)), ((), ())),
            preferred_element_type=jnp.float32,
        )
        for side in range(2):
            spot = pl.ds(step * each + item + side * pair, slots, stride=share)
            mine = value[side * HALF : side * HALF + slots, side * width : (side + 1) * width]
            for part in range(2):
                summed[part, spot, :] = mine[:, part * LANES : (part + 1) * LANES]

    @pl.when(step == pair // each - 1)
    def _round():
        for part in range(2):
            out[:, :, part * LANES : (part + 1) * LANES] = (
                summed[part].reshape(slots, share, LANES).astype(jnp.bfloat16)
            )


def encode(received, phases, before, chunk, half, cap, freq_block, shots):
    sources = received.shape[0]
    share = freq_block // HALVES
    pair = share // 2
    each = 2
    group = 2 * shots
    held = received.reshape(sources, -1, group, LANES)
    slots = min(cap, HALF)
    depth = phases.shape[1]
    in_specs = [
        pl.BlockSpec((sources, each, group, LANES), lambda i: (0, i, 0, 0)),
        pl.BlockSpec((each, depth, 4 * RAY_PARAM_COUNT), lambda i: (i, 0, 0)),
    ]
    operands = [held, phases]
    aliases = {}
    if before is not None:
        in_specs.append(pl.BlockSpec(memory_space=pl.ANY))
        operands.append(before)
        aliases = {2: 0}
    return pl.pallas_call(
        functools.partial(encode_kernel, slots, pair, each),
        grid=(pair // each,),
        in_specs=in_specs,
        out_specs=pl.BlockSpec((slots, share, 2 * RAY_PARAM_COUNT), lambda i: (chunk, half, 0)),
        out_shape=jax.ShapeDtypeStruct((cap, freq_block, 2 * RAY_PARAM_COUNT), jnp.bfloat16),
        scratch_shapes=[pltpu.VMEM((2, slots * share, LANES), jnp.float32)],
        input_output_aliases=aliases,
        compiler_params=pltpu.CompilerParams(vmem_limit_bytes=VMEM_BYTES),
        cost_estimate=pl.CostEstimate(
            flops=2 * share * depth * LANES * 2 * RAY_PARAM_COUNT,
            bytes_accessed=16 * 1024 * 1024,
            transcendentals=0,
        ),
        name="encode",
    )(*operands)


def on_device(traces, trace_counts, aperture_start, shot_position, rec_slot):
    shots = trace_counts.shape[1]
    freq_groups = lax.axis_size("freq")
    slabs = lax.axis_size("slab")
    freq_block = FREQUENCY_COUNT // freq_groups
    share = freq_block // HALVES
    cap = 3 * NREC // (2 * slabs)
    chunks = -(-cap // HALF)
    assert cap % min(cap, HALF) == 0
    counts = trace_counts[0]
    inverses = [chunk_inverse(rec_slot, slabs, cap, chunk) for chunk in range(chunks)]
    own_bin = F0 + lax.axis_index("freq") * freq_block
    first_bins = [(own_bin + half * share).astype(jnp.int32)[None] for half in range(HALVES)]
    parts = [(half, chunk) for half in range(HALVES) for chunk in range(chunks)]

    def first_of(half, traces):
        return first_chunk(
            traces, counts, aperture_start, shot_position, inverses[0], slabs, freq_groups, half
        )

    def later_of(spectra, chunk):
        return later_chunk(
            spectra, counts, aperture_start, inverses[chunk], slabs, freq_groups
        )

    spectra, sent = first_of(0, traces)
    phases = [None] * HALVES
    encoded = None
    received = exchange(sent)
    upcoming = None
    for index, (half, chunk) in enumerate(parts):
        if index + 1 < len(parts):
            next_half, next_chunk = parts[index + 1]
            if next_chunk == 0:
                spectra, sent = first_of(next_half, traces)
            else:
                sent = later_of(spectra, next_chunk)
            tied = (received, sent) + (() if encoded is None else (encoded,))
            tied = lax.optimization_barrier(tied)
            received, sent = tied[:2]
            encoded = tied[2] if encoded is not None else None
            upcoming = exchange(sent)
        if index == 0:
            for h in range(HALVES):
                phases[h] = make_phases(received, first_bins[h], share // 2, shots)
        encoded = encode(received, phases[half], encoded, chunk, half, cap, freq_block, shots)
        received = upcoming
    return encoded


def exchange(sent):
    return lax.all_to_all(sent, ("freq", "slab"), split_axis=0, concat_axis=0, tiled=True)


def solution(mesh):
    return jax.shard_map(
        on_device,
        mesh=mesh,
        in_specs=(
            P(("freq", "slab"), None),
            P(("freq", "slab"), None),
            P(("freq", "slab")),
            P(("freq", "slab")),
            P(),
        ),
        out_specs=P("slab", "freq", None),
        check_vma=False,
    )
```

```python
import functools
import math

import jax
import jax.numpy as jnp
import ml_dtypes
import numpy as np
from jax import lax
from jax.experimental import pallas as pl
from jax.experimental.pallas import tpu as pltpu
from jax.sharding import PartitionSpec as P

NT = 2048
FREQUENCY_COUNT = 256
F0 = 8
RAY_PARAM_COUNT = 128
NREC = 512
RDIV = 16
LANES = 128
HALF = 64
HALVES = 2
BINS = FREQUENCY_COUNT // HALVES
VMEM_BYTES = 56 * 1024 * 1024


def dft_table(samples, freq_groups, half):
    share = FREQUENCY_COUNT // freq_groups // HALVES
    owners = np.arange(freq_groups, dtype=np.int64)[:, None] * (HALVES * share)
    bins = (F0 + owners + half * share + np.arange(share, dtype=np.int64)[None, :]).reshape(-1)
    index = (np.arange(samples, dtype=np.int64)[:, None] * bins[None, :]) % samples
    angle = index.astype(np.float64) * (2.0 * math.pi / samples)
    factor = 1.0 / math.sqrt(samples)
    table = np.concatenate([np.cos(angle), -np.sin(angle)], axis=1) * factor
    return table.astype(np.float32).astype(ml_dtypes.bfloat16)


def chunk_columns(slabs, cap, chunk):
    lane = chunk * HALF + np.arange(HALF)
    slots = [np.where(lane < cap, slab * cap + lane, -2) for slab in range(slabs)]
    return np.concatenate(slots).astype(np.int32)


def place(slabs, freq_groups, shots, chunk, segment, starts, counts, inverse, spectra, out, part):
    total = spectra.shape[1]
    window = NREC + LANES
    pair = BINS // freq_groups // 2
    lane = lax.broadcasted_iota(jnp.int32, (BINS // 2, LANES), 1)

    def one_shot(k, begin):
        base = pl.multiple_of(jnp.minimum((begin // LANES) * LANES, total - window), LANES)
        piece = spectra[:, pl.ds(base, window)]
        for first in range(0, slabs * HALF, 2 * LANES):
            inv = inverse[chunk : chunk + 1, first : first + 2 * LANES]
            offset = jnp.bitwise_and(inv - starts[k], NREC - 1)
            valid = (inv >= 0) & (offset < counts[k])
            target = jnp.where(valid, offset + (begin - base), -1)
            line = lax.broadcasted_iota(jnp.int32, (window, 2 * LANES), 0)
            hot = jnp.where(line == target, 1.0, 0.0).astype(jnp.bfloat16)
            placed = jnp.dot(piece, hot, preferred_element_type=jnp.float32)
            for half in range(2):
                slab = (first + half * LANES) // HALF
                value = placed[:, half * LANES : (half + 1) * LANES]
                for c in range(2):
                    mine = value[c * BINS : (c + 1) * BINS]
                    split = mine.reshape(freq_groups, 2, pair, LANES)
                    low = split[:, 0].reshape(freq_groups * pair, LANES)
                    high = split[:, 1].reshape(freq_groups * pair, LANES)
                    spot = pl.ds(c * shots + k, freq_groups * pair, stride=2 * shots)
                    part[slab, spot, :] = jnp.where(lane < HALF, low, pltpu.roll(high, HALF, 1))
                    part[slab + 1, spot, :] = jnp.where(lane < HALF, pltpu.roll(low, HALF, 1), high)
        return begin + counts[k]

    lax.fori_loop(0, shots, one_shot, 0)
    rows = pair * 2 * shots

    def deliver(group, carry):
        for slab in range(slabs):
            out[group * slabs + slab, segment * rows : (segment + 1) * rows, :] = part[
                slab, pl.ds(pl.multiple_of(group * rows, rows), rows), :
            ].astype(jnp.bfloat16)
        return carry

    lax.fori_loop(0, freq_groups, deliver, 0)


def stage_kernel(
    slabs, freq_groups, shots, row_steps, fresh, parts, with_positions,
    starts, counts, positions, inverse, *refs,
):
    refs = list(refs)
    part = refs.pop()
    step = pl.program_id(0)
    spectra = {}
    if fresh is not None:
        table, traces = refs[:2]
        mine, out = refs[-2:]
        known = refs[2:-2]
        spectra[fresh] = mine
        rows = traces.shape[0]
        block = jnp.dot(traces[...], table[...], preferred_element_type=jnp.float32)
        mine[:, pl.ds(pl.multiple_of(step * rows, rows), rows)] = block.T.astype(jnp.bfloat16)
    else:
        out = refs[-1]
        known = refs[:-1]
    for half, ref in zip(sorted({h for h, _ in parts} - {fresh}), known):
        spectra[half] = ref

    @pl.when(step == row_steps - 1)
    def _place():
        for segment, (half, chunk) in enumerate(parts):
            place(
                slabs, freq_groups, shots, chunk, segment,
                starts, counts, inverse, spectra[half], out, part,
            )
        if not with_positions:
            return
        line = lax.broadcasted_iota(jnp.int32, (2 * shots, LANES), 0)
        halves = jnp.zeros((2 * shots, LANES), jnp.int32)
        for k in range(shots):
            halves = jnp.where(line == k, positions[k] // HALF, halves)
            halves = jnp.where(line == shots + k, positions[k] % HALF, halves)
        coded = halves.astype(jnp.float32).astype(jnp.bfloat16)
        rows_used = out.shape[1] - 2 * shots
        for dest in range(out.shape[0]):
            out[dest, rows_used:, :] = coded


def stage(
    traces, counts, starts, positions, inverse, slabs, freq_groups,
    fresh, parts, spectra, with_positions,
):
    row_total, samples = traces.shape
    shots = counts.shape[0]
    rows = 512
    row_steps = row_total // rows if fresh is not None else 1
    dests = freq_groups * slabs
    dest_rows = BINS // freq_groups // 2 * 2 * shots * len(parts)
    dest_rows += 2 * shots if with_positions else 0
    smem = pl.BlockSpec(memory_space=pltpu.SMEM)
    whole = pl.BlockSpec((2 * BINS, row_total), lambda i: (0, 0))
    shape = jax.ShapeDtypeStruct((2 * BINS, row_total), jnp.bfloat16)
    in_specs = [smem, smem, smem, pl.BlockSpec(inverse.shape, lambda i: (0, 0))]
    operands = [starts, counts, positions, inverse]
    out_specs = [pl.BlockSpec((dests, dest_rows, LANES), lambda i: (0, 0, 0))]
    out_shape = [jax.ShapeDtypeStruct((dests, dest_rows, LANES), jnp.bfloat16)]
    flops = len(parts) * 2 * 2 * BINS * shots * (NREC + LANES) * slabs * HALF
    if fresh is not None:
        in_specs += [
            pl.BlockSpec((samples, 2 * BINS), lambda i: (0, 0)),
            pl.BlockSpec((rows, samples), lambda i: (i, 0)),
        ]
        operands += [jnp.asarray(dft_table(samples, freq_groups, fresh)), traces]
        out_specs = [whole] + out_specs
        out_shape = [shape] + out_shape
        flops += 2 * row_total * samples * 2 * BINS
    for half in sorted({h for h, _ in parts} - {fresh}):
        in_specs.append(whole)
        operands.append(spectra[half])
    result = pl.pallas_call(
        functools.partial(
            stage_kernel, slabs, freq_groups, shots, row_steps, fresh, parts, with_positions
        ),
        grid=(row_steps,),
        in_specs=in_specs,
        out_specs=out_specs,
        out_shape=out_shape,
        scratch_shapes=[pltpu.VMEM((slabs, BINS * shots, LANES), jnp.float32)],
        compiler_params=pltpu.CompilerParams(vmem_limit_bytes=VMEM_BYTES),
        cost_estimate=pl.CostEstimate(
            flops=flops, bytes_accessed=row_total * samples * 2, transcendentals=0
        ),
        name="stage",
    )(*operands)
    if fresh is not None:
        spectra[fresh] = result[0]
    return result[-1]


def chunk_inverse(rec_slot, slabs, cap, chunk):
    slots = jnp.asarray(chunk_columns(slabs, cap, chunk))
    receivers = jnp.arange(NREC, dtype=jnp.int32)
    return jnp.max(
        jnp.where(rec_slot[:, None] == slots[None, :], receivers[:, None], -1), axis=0
    )


def cos_sin(q, period):
    quarter = period // 4
    shifted = q + quarter // 2
    quadrant = jnp.bitwise_and(shifted // quarter, 3)
    x = (jnp.bitwise_and(shifted, quarter - 1) - quarter // 2).astype(jnp.float32) * (
        2.0 * math.pi / period
    )
    x2 = x * x
    sine = x + x * x2 * (
        -1.6666666666e-1 + x2 * (8.3333333e-3 + x2 * (-1.98412698e-4 + x2 * 2.7557319e-6))
    )
    cosine = 1.0 + x2 * (
        -0.5 + x2 * (4.16666667e-2 + x2 * (-1.38888889e-3 + x2 * 2.48015873e-5))
    )
    swap = jnp.bitwise_and(quadrant, 1) == 1
    c = jnp.where(swap, sine, cosine)
    s = jnp.where(swap, cosine, sine)
    c = jnp.where((quadrant == 1) | (quadrant == 2), -c, c)
    s = jnp.where(quadrant >= 2, -s, s)
    return c, s


def phase_kernel(shots, total_shots, pair, first_bin, halves, out):
    sources = halves.shape[0]
    coded = halves[...].reshape(sources, 2 * shots, LANES).astype(jnp.float32)
    positions = (coded[:, :shots] * HALF + coded[:, shots:]).astype(jnp.int32)
    rays = lax.broadcasted_iota(jnp.int32, positions.shape, 2) - RAY_PARAM_COUNT // 2
    period = NT * RDIV
    factor = 1.0 / math.sqrt(total_shots)
    for side in range(2):
        bin_index = first_bin[0] + pl.program_id(0) + side * pair
        q = jnp.bitwise_and(bin_index * rays * positions, period - 1)
        c, s = cos_sin(q, period)
        c = (c * factor)[:, None]
        s = (s * factor)[:, None]
        left = jnp.concatenate([c, s], axis=1).reshape(sources * 2 * shots, RAY_PARAM_COUNT)
        right = jnp.concatenate([-s, c], axis=1).reshape(sources * 2 * shots, RAY_PARAM_COUNT)
        at = 2 * side * RAY_PARAM_COUNT
        out[0, :, at : at + RAY_PARAM_COUNT] = left.astype(jnp.bfloat16)
        out[0, :, at + RAY_PARAM_COUNT : at + 2 * RAY_PARAM_COUNT] = right.astype(jnp.bfloat16)


def make_phases(received, first_bin, pair, shots):
    sources = received.shape[0]
    total_shots = sources * shots
    held = received.reshape(sources, -1, 2 * shots, LANES)
    last = held.shape[1] - 1
    return pl.pallas_call(
        functools.partial(phase_kernel, shots, total_shots, pair),
        grid=(pair,),
        in_specs=[
            pl.BlockSpec(memory_space=pltpu.SMEM),
            pl.BlockSpec((sources, 1, 2 * shots, LANES), lambda i: (0, last, 0, 0)),
        ],
        out_specs=pl.BlockSpec((1, 2 * total_shots, 4 * RAY_PARAM_COUNT), lambda i: (i, 0, 0)),
        out_shape=jax.ShapeDtypeStruct(
            (pair, 2 * total_shots, 4 * RAY_PARAM_COUNT), jnp.bfloat16
        ),
        compiler_params=pltpu.CompilerParams(vmem_limit_bytes=VMEM_BYTES),
        cost_estimate=pl.CostEstimate(
            flops=pair * total_shots * RAY_PARAM_COUNT * 80,
            bytes_accessed=32 * 1024 * 1024,
            transcendentals=0,
        ),
        name="phases",
    )(first_bin, held)


def encode_kernel(slots, pair, each, *refs):
    held, phases = refs[:2]
    out, summed = refs[-2:]
    step = pl.program_id(0)
    share = 2 * pair
    depth = phases.shape[1]
    width = 2 * RAY_PARAM_COUNT
    for item in range(each):
        value = lax.dot_general(
            held[:, item].reshape(depth, LANES),
            phases[item],
            (((0,), (0,)), ((), ())),
            preferred_element_type=jnp.float32,
        )
        for side in range(2):
            spot = pl.ds(step * each + item + side * pair, slots, stride=share)
            mine = value[side * HALF : side * HALF + slots, side * width : (side + 1) * width]
            for part in range(2):
                summed[part, spot, :] = mine[:, part * LANES : (part + 1) * LANES]

    @pl.when(step == pair // each - 1)
    def _round():
        for part in range(2):
            out[:, :, part * LANES : (part + 1) * LANES] = (
                summed[part].reshape(slots, share, LANES).astype(jnp.bfloat16)
            )


def encode(received, phases, before, segment, chunk, half, cap, freq_block, shots):
    sources = received.shape[0]
    share = freq_block // HALVES
    pair = share // 2
    each = 2
    group = 2 * shots
    held = received.reshape(sources, -1, group, LANES)
    slots = min(cap, HALF)
    depth = phases.shape[1]
    in_specs = [
        pl.BlockSpec(
            (sources, each, group, LANES), lambda i: (0, segment * (pair // each) + i, 0, 0)
        ),
        pl.BlockSpec((each, depth, 4 * RAY_PARAM_COUNT), lambda i: (i, 0, 0)),
    ]
    operands = [held, phases]
    aliases = {}
    if before is not None:
        in_specs.append(pl.BlockSpec(memory_space=pl.ANY))
        operands.append(before)
        aliases = {2: 0}
    return pl.pallas_call(
        functools.partial(encode_kernel, slots, pair, each),
        grid=(pair // each,),
        in_specs=in_specs,
        out_specs=pl.BlockSpec((slots, share, 2 * RAY_PARAM_COUNT), lambda i: (chunk, half, 0)),
        out_shape=jax.ShapeDtypeStruct((cap, freq_block, 2 * RAY_PARAM_COUNT), jnp.bfloat16),
        scratch_shapes=[pltpu.VMEM((2, slots * share, LANES), jnp.float32)],
        input_output_aliases=aliases,
        compiler_params=pltpu.CompilerParams(vmem_limit_bytes=VMEM_BYTES),
        cost_estimate=pl.CostEstimate(
            flops=2 * share * depth * LANES * 2 * RAY_PARAM_COUNT,
            bytes_accessed=16 * 1024 * 1024,
            transcendentals=0,
        ),
        name="encode",
    )(*operands)


def on_device(traces, trace_counts, aperture_start, shot_position, rec_slot):
    shots = trace_counts.shape[1]
    freq_groups = lax.axis_size("freq")
    slabs = lax.axis_size("slab")
    freq_block = FREQUENCY_COUNT // freq_groups
    share = freq_block // HALVES
    cap = 3 * NREC // (2 * slabs)
    chunks = -(-cap // HALF)
    assert cap % min(cap, HALF) == 0
    counts = trace_counts[0]
    inverse = jnp.stack([chunk_inverse(rec_slot, slabs, cap, chunk) for chunk in range(chunks)])
    own_bin = F0 + lax.axis_index("freq") * freq_block
    first_bins = [(own_bin + half * share).astype(jnp.int32)[None] for half in range(HALVES)]
    order = [(half, chunk) for half in range(HALVES) for chunk in range(chunks)]
    groups = [order[:1], order[1:-1], order[-1:]]
    groups = [group for group in groups if group]
    spectra = {}

    def make(index):
        missing = [h for h, _ in groups[index] if h not in spectra]
        return stage(
            traces, counts, aperture_start, shot_position, inverse, slabs, freq_groups,
            missing[0] if missing else None, groups[index], spectra, index == 0,
        )

    phases, encoded = None, None
    received = exchange(make(0))
    for index, group in enumerate(groups):
        upcoming = None
        if index + 1 < len(groups):
            tied = (received, make(index + 1)) + (() if encoded is None else (encoded,))
            tied = lax.optimization_barrier(tied)
            received = tied[0]
            encoded = tied[2] if encoded is not None else None
            upcoming = exchange(tied[1])
        if index == 0:
            phases = [make_phases(received, first, share // 2, shots) for first in first_bins]
        for segment, (half, chunk) in enumerate(group):
            encoded = encode(
                received, phases[half], encoded, segment, chunk, half, cap, freq_block, shots
            )
        received = upcoming
    return encoded


def exchange(sent):
    return lax.all_to_all(sent, ("freq", "slab"), split_axis=0, concat_axis=0, tiled=True)


def solution(mesh):
    return jax.shard_map(
        on_device,
        mesh=mesh,
        in_specs=(
            P(("freq", "slab"), None),
            P(("freq", "slab"), None),
            P(("freq", "slab")),
            P(("freq", "slab")),
            P(),
        ),
        out_specs=P("slab", "freq", None),
        check_vma=False,
    )
```

```python
import functools
import math

import jax
import jax.numpy as jnp
import ml_dtypes
import numpy as np
from jax import lax
from jax.experimental import pallas as pl
from jax.experimental.pallas import tpu as pltpu
from jax.sharding import PartitionSpec as P

NT = 2048
FREQUENCY_COUNT = 256
F0 = 8
RAY_PARAM_COUNT = 128
NREC = 512
RDIV = 16
LANES = 128
HALF = 64
HALVES = 2
BINS = FREQUENCY_COUNT // HALVES
VMEM_BYTES = 63 * 1024 * 1024


def dft_table(samples, freq_groups, half):
    share = FREQUENCY_COUNT // freq_groups // HALVES
    owners = np.arange(freq_groups, dtype=np.int64)[:, None] * (HALVES * share)
    bins = (F0 + owners + half * share + np.arange(share, dtype=np.int64)[None, :]).reshape(-1)
    index = (np.arange(samples, dtype=np.int64)[:, None] * bins[None, :]) % samples
    angle = index.astype(np.float64) * (2.0 * math.pi / samples)
    factor = 1.0 / math.sqrt(samples)
    table = np.concatenate([np.cos(angle), -np.sin(angle)], axis=1) * factor
    return table.astype(np.float32).astype(ml_dtypes.bfloat16)


def chunk_columns(slabs, cap, chunk):
    lane = chunk * HALF + np.arange(HALF)
    slots = [np.where(lane < cap, slab * cap + lane, -2) for slab in range(slabs)]
    return np.concatenate(slots).astype(np.int32)


def place(slabs, freq_groups, shots, chunk, segment, starts, counts, inverse, spectra, out, part):
    total = spectra.shape[1]
    window = NREC + LANES
    pair = BINS // freq_groups // 2
    lane = lax.broadcasted_iota(jnp.int32, (BINS // 2, LANES), 1)

    def one_shot(k, begin):
        base = pl.multiple_of(jnp.minimum((begin // LANES) * LANES, total - window), LANES)
        piece = spectra[:, pl.ds(base, window)]
        for first in range(0, slabs * HALF, 2 * LANES):
            at = chunk * slabs * HALF + first
            inv = inverse[:, at : at + 2 * LANES]
            offset = jnp.bitwise_and(inv - starts[k], NREC - 1)
            valid = (inv >= 0) & (offset < counts[k])
            target = jnp.where(valid, offset + (begin - base), -1)
            line = lax.broadcasted_iota(jnp.int32, (window, 2 * LANES), 0)
            hot = jnp.where(line == target, 1.0, 0.0).astype(jnp.bfloat16)
            placed = jnp.dot(piece, hot, preferred_element_type=jnp.float32)
            for half in range(2):
                slab = (first + half * LANES) // HALF
                value = placed[:, half * LANES : (half + 1) * LANES]
                for c in range(2):
                    mine = value[c * BINS : (c + 1) * BINS]
                    split = mine.reshape(freq_groups, 2, pair, LANES)
                    low = split[:, 0].reshape(freq_groups * pair, LANES)
                    high = split[:, 1].reshape(freq_groups * pair, LANES)
                    spot = pl.ds(c * shots + k, freq_groups * pair, stride=2 * shots)
                    part[slab, spot, :] = jnp.where(lane < HALF, low, pltpu.roll(high, HALF, 1))
                    part[slab + 1, spot, :] = jnp.where(lane < HALF, pltpu.roll(low, HALF, 1), high)
        return begin + counts[k]

    lax.fori_loop(0, shots, one_shot, 0, unroll=True)
    rows = pair * 2 * shots

    def deliver(group, carry):
        for slab in range(slabs):
            out[group * slabs + slab, segment * rows : (segment + 1) * rows, :] = part[
                slab, pl.ds(pl.multiple_of(group * rows, rows), rows), :
            ].astype(jnp.bfloat16)
        return carry

    lax.fori_loop(0, freq_groups, deliver, 0)


def stage_kernel(
    slabs, freq_groups, shots, row_steps, fresh, parts, with_positions,
    starts, counts, positions, inverse, *refs,
):
    refs = list(refs)
    part = refs.pop()
    step = pl.program_id(0)
    spectra = {}
    if fresh is not None:
        table, traces = refs[:2]
        mine, out = refs[-2:]
        known = refs[2:-2]
        spectra[fresh] = mine
        rows = traces.shape[0]
        block = jnp.dot(traces[...], table[...], preferred_element_type=jnp.float32)
        mine[:, pl.ds(pl.multiple_of(step * rows, rows), rows)] = block.astype(jnp.bfloat16).T
    else:
        out = refs[-1]
        known = refs[:-1]
    for half, ref in zip(sorted({h for h, _ in parts} - {fresh}), known):
        spectra[half] = ref

    @pl.when(step == row_steps - 1)
    def _place():
        for segment, (half, chunk) in enumerate(parts):
            place(
                slabs, freq_groups, shots, chunk, segment,
                starts, counts, inverse, spectra[half], out, part,
            )
        if not with_positions:
            return
        line = lax.broadcasted_iota(jnp.int32, (2 * shots, LANES), 0)
        halves = jnp.zeros((2 * shots, LANES), jnp.int32)
        for k in range(shots):
            halves = jnp.where(line == k, positions[k] // HALF, halves)
            halves = jnp.where(line == shots + k, positions[k] % HALF, halves)
        coded = halves.astype(jnp.float32).astype(jnp.bfloat16)
        rows_used = out.shape[1] - 2 * shots
        for dest in range(out.shape[0]):
            out[dest, rows_used:, :] = coded


def stage(
    traces, counts, starts, positions, inverse, slabs, freq_groups,
    fresh, parts, spectra, with_positions,
):
    row_total, samples = traces.shape
    shots = counts.shape[0]
    rows = 512
    row_steps = row_total // rows if fresh is not None else 1
    dests = freq_groups * slabs
    dest_rows = BINS // freq_groups // 2 * 2 * shots * len(parts)
    dest_rows += 2 * shots if with_positions else 0
    smem = pl.BlockSpec(memory_space=pltpu.SMEM)
    whole = pl.BlockSpec((2 * BINS, row_total), lambda i: (0, 0))
    shape = jax.ShapeDtypeStruct((2 * BINS, row_total), jnp.bfloat16)
    in_specs = [smem, smem, smem, pl.BlockSpec(inverse.shape, lambda i: (0, 0))]
    operands = [starts, counts, positions, inverse]
    out_specs = [pl.BlockSpec((dests, dest_rows, LANES), lambda i: (0, 0, 0))]
    out_shape = [jax.ShapeDtypeStruct((dests, dest_rows, LANES), jnp.bfloat16)]
    flops = len(parts) * 2 * 2 * BINS * shots * (NREC + LANES) * slabs * HALF
    if fresh is not None:
        in_specs += [
            pl.BlockSpec((samples, 2 * BINS), lambda i: (0, 0)),
            pl.BlockSpec((rows, samples), lambda i: (i, 0)),
        ]
        operands += [jnp.asarray(dft_table(samples, freq_groups, fresh)), traces]
        out_specs = [whole] + out_specs
        out_shape = [shape] + out_shape
        flops += 2 * row_total * samples * 2 * BINS
    for half in sorted({h for h, _ in parts} - {fresh}):
        in_specs.append(whole)
        operands.append(spectra[half])
    result = pl.pallas_call(
        functools.partial(
            stage_kernel, slabs, freq_groups, shots, row_steps, fresh, parts, with_positions
        ),
        grid=(row_steps,),
        in_specs=in_specs,
        out_specs=out_specs,
        out_shape=out_shape,
        scratch_shapes=[pltpu.VMEM((slabs, BINS * shots, LANES), jnp.float32)],
        compiler_params=pltpu.CompilerParams(vmem_limit_bytes=VMEM_BYTES),
        cost_estimate=pl.CostEstimate(
            flops=flops, bytes_accessed=row_total * samples * 2, transcendentals=0
        ),
        name="stage",
    )(*operands)
    if fresh is not None:
        spectra[fresh] = result[0]
    return result[-1]


def inverse_table(rec_slot, slabs, cap, chunks):
    slots = np.concatenate([chunk_columns(slabs, cap, chunk) for chunk in range(chunks)])
    receivers = jnp.arange(NREC, dtype=jnp.int32)
    return jnp.max(
        jnp.where(rec_slot[:, None] == jnp.asarray(slots)[None, :], receivers[:, None], -1), axis=0
    )[None, :]


def cos_sin(q, period):
    quarter = period // 4
    shifted = q + quarter // 2
    quadrant = jnp.bitwise_and(shifted // quarter, 3)
    x = (jnp.bitwise_and(shifted, quarter - 1) - quarter // 2).astype(jnp.float32) * (
        2.0 * math.pi / period
    )
    x2 = x * x
    sine = x + x * x2 * (
        -1.6666666666e-1 + x2 * (8.3333333e-3 + x2 * (-1.98412698e-4 + x2 * 2.7557319e-6))
    )
    cosine = 1.0 + x2 * (
        -0.5 + x2 * (4.16666667e-2 + x2 * (-1.38888889e-3 + x2 * 2.48015873e-5))
    )
    swap = jnp.bitwise_and(quadrant, 1) == 1
    c = jnp.where(swap, sine, cosine)
    s = jnp.where(swap, cosine, sine)
    c = jnp.where((quadrant == 1) | (quadrant == 2), -c, c)
    s = jnp.where(quadrant >= 2, -s, s)
    return c, s


def phase_kernel(shots, total_shots, pair, first_bin, halves, out):
    sources = halves.shape[0]
    coded = halves[...].reshape(sources, 2 * shots, LANES).astype(jnp.float32)
    positions = (coded[:, :shots] * HALF + coded[:, shots:]).astype(jnp.int32)
    rays = lax.broadcasted_iota(jnp.int32, positions.shape, 2) - RAY_PARAM_COUNT // 2
    period = NT * RDIV
    factor = 1.0 / math.sqrt(total_shots)
    for side in range(2):
        bin_index = first_bin[0] + pl.program_id(0) + side * pair
        q = jnp.bitwise_and(bin_index * rays * positions, period - 1)
        c, s = cos_sin(q, period)
        c = (c * factor)[:, None]
        s = (s * factor)[:, None]
        left = jnp.concatenate([c, s], axis=1).reshape(sources * 2 * shots, RAY_PARAM_COUNT)
        right = jnp.concatenate([-s, c], axis=1).reshape(sources * 2 * shots, RAY_PARAM_COUNT)
        at = 2 * side * RAY_PARAM_COUNT
        out[0, :, at : at + RAY_PARAM_COUNT] = left.astype(jnp.bfloat16)
        out[0, :, at + RAY_PARAM_COUNT : at + 2 * RAY_PARAM_COUNT] = right.astype(jnp.bfloat16)


def make_phases(received, first_bin, pair, shots):
    sources = received.shape[0]
    total_shots = sources * shots
    held = received.reshape(sources, -1, 2 * shots, LANES)
    last = held.shape[1] - 1
    return pl.pallas_call(
        functools.partial(phase_kernel, shots, total_shots, pair),
        grid=(pair,),
        in_specs=[
            pl.BlockSpec(memory_space=pltpu.SMEM),
            pl.BlockSpec((sources, 1, 2 * shots, LANES), lambda i: (0, last, 0, 0)),
        ],
        out_specs=pl.BlockSpec((1, 2 * total_shots, 4 * RAY_PARAM_COUNT), lambda i: (i, 0, 0)),
        out_shape=jax.ShapeDtypeStruct(
            (pair, 2 * total_shots, 4 * RAY_PARAM_COUNT), jnp.bfloat16
        ),
        compiler_params=pltpu.CompilerParams(vmem_limit_bytes=VMEM_BYTES),
        cost_estimate=pl.CostEstimate(
            flops=pair * total_shots * RAY_PARAM_COUNT * 80,
            bytes_accessed=32 * 1024 * 1024,
            transcendentals=0,
        ),
        name="phases",
    )(first_bin, held)


def encode_kernel(slots, pair, each, *refs):
    held, phases = refs[:2]
    out, summed = refs[-2:]
    step = pl.program_id(0)
    share = 2 * pair
    depth = phases.shape[1]
    width = 2 * RAY_PARAM_COUNT
    for item in range(each):
        value = lax.dot_general(
            held[:, item].reshape(depth, LANES),
            phases[item],
            (((0,), (0,)), ((), ())),
            preferred_element_type=jnp.float32,
        )
        for side in range(2):
            spot = pl.ds(step * each + item + side * pair, slots, stride=share)
            mine = value[side * HALF : side * HALF + slots, side * width : (side + 1) * width]
            for part in range(2):
                summed[part, spot, :] = mine[:, part * LANES : (part + 1) * LANES]

    @pl.when(step == pair // each - 1)
    def _round():
        for part in range(2):
            out[:, :, part * LANES : (part + 1) * LANES] = (
                summed[part].reshape(slots, share, LANES).astype(jnp.bfloat16)
            )


def encode(received, phases, before, segment, chunk, half, cap, freq_block, shots):
    sources = received.shape[0]
    share = freq_block // HALVES
    pair = share // 2
    each = 2
    group = 2 * shots
    held = received.reshape(sources, -1, group, LANES)
    slots = min(cap, HALF)
    depth = phases.shape[1]
    in_specs = [
        pl.BlockSpec(
            (sources, each, group, LANES), lambda i: (0, segment * (pair // each) + i, 0, 0)
        ),
        pl.BlockSpec((each, depth, 4 * RAY_PARAM_COUNT), lambda i: (i, 0, 0)),
    ]
    operands = [held, phases]
    aliases = {}
    if before is not None:
        in_specs.append(pl.BlockSpec(memory_space=pl.ANY))
        operands.append(before)
        aliases = {2: 0}
    return pl.pallas_call(
        functools.partial(encode_kernel, slots, pair, each),
        grid=(pair // each,),
        in_specs=in_specs,
        out_specs=pl.BlockSpec((slots, share, 2 * RAY_PARAM_COUNT), lambda i: (chunk, half, 0)),
        out_shape=jax.ShapeDtypeStruct((cap, freq_block, 2 * RAY_PARAM_COUNT), jnp.bfloat16),
        scratch_shapes=[pltpu.VMEM((2, slots * share, LANES), jnp.float32)],
        input_output_aliases=aliases,
        compiler_params=pltpu.CompilerParams(vmem_limit_bytes=VMEM_BYTES),
        cost_estimate=pl.CostEstimate(
            flops=2 * share * depth * LANES * 2 * RAY_PARAM_COUNT,
            bytes_accessed=16 * 1024 * 1024,
            transcendentals=0,
        ),
        name="encode",
    )(*operands)


def on_device(traces, trace_counts, aperture_start, shot_position, rec_slot):
    shots = trace_counts.shape[1]
    freq_groups = lax.axis_size("freq")
    slabs = lax.axis_size("slab")
    freq_block = FREQUENCY_COUNT // freq_groups
    share = freq_block // HALVES
    cap = 3 * NREC // (2 * slabs)
    chunks = -(-cap // HALF)
    assert cap % min(cap, HALF) == 0
    counts = trace_counts[0]
    inverse = inverse_table(rec_slot, slabs, cap, chunks)
    own_bin = F0 + lax.axis_index("freq") * freq_block
    first_bins = [(own_bin + half * share).astype(jnp.int32)[None] for half in range(HALVES)]
    order = [(half, chunk) for half in range(HALVES) for chunk in range(chunks)]
    groups = [order[:1], order[1:-1], order[-1:]]
    groups = [group for group in groups if group]
    spectra = {}

    def make(index):
        missing = [h for h, _ in groups[index] if h not in spectra]
        return stage(
            traces, counts, aperture_start, shot_position, inverse, slabs, freq_groups,
            missing[0] if missing else None, groups[index], spectra, index == 0,
        )

    phases, encoded = None, None
    received = exchange(make(0))
    for index, group in enumerate(groups):
        upcoming = None
        if index + 1 < len(groups):
            tied = lax.optimization_barrier((received, make(index + 1), phases, encoded))
            received, sent, phases, encoded = tied
            upcoming = exchange(sent)
        if index == 0:
            phases = [make_phases(received, first, share // 2, shots) for first in first_bins]
        for segment, (half, chunk) in enumerate(group):
            encoded = encode(
                received, phases[half], encoded, segment, chunk, half, cap, freq_block, shots
            )
        received = upcoming
    return encoded


def exchange(sent):
    return lax.all_to_all(sent, ("freq", "slab"), split_axis=0, concat_axis=0, tiled=True)


def solution(mesh):
    return jax.shard_map(
        on_device,
        mesh=mesh,
        in_specs=(
            P(("freq", "slab"), None),
            P(("freq", "slab"), None),
            P(("freq", "slab")),
            P(("freq", "slab")),
            P(),
        ),
        out_specs=P("slab", "freq", None),
        check_vma=False,
    )
```

```python
import functools
import math

import jax
import jax.numpy as jnp
import ml_dtypes
import numpy as np
from jax import lax
from jax.experimental import pallas as pl
from jax.experimental.pallas import tpu as pltpu
from jax.sharding import PartitionSpec as P

NT = 2048
FREQUENCY_COUNT = 256
F0 = 8
RAY_PARAM_COUNT = 128
NREC = 512
RDIV = 16
LANES = 128
HALF = 64
HALVES = 2
BINS = FREQUENCY_COUNT // HALVES
VMEM_BYTES = 63 * 1024 * 1024


def dft_table(samples, freq_groups, half):
    share = FREQUENCY_COUNT // freq_groups // HALVES
    owners = np.arange(freq_groups, dtype=np.int64)[:, None] * (HALVES * share)
    bins = (F0 + owners + half * share + np.arange(share, dtype=np.int64)[None, :]).reshape(-1)
    index = (np.arange(samples, dtype=np.int64)[:, None] * bins[None, :]) % samples
    angle = index.astype(np.float64) * (2.0 * math.pi / samples)
    factor = 1.0 / math.sqrt(samples)
    table = np.concatenate([np.cos(angle), -np.sin(angle)], axis=1) * factor
    return table.astype(np.float32).astype(ml_dtypes.bfloat16)


def chunk_columns(slabs, cap, chunk):
    lane = chunk * HALF + np.arange(HALF)
    slots = [np.where(lane < cap, slab * cap + lane, -2) for slab in range(slabs)]
    return np.concatenate(slots).astype(np.int32)


def place(slabs, freq_groups, shots, chunk, segment, starts, counts, inverse, spectra, out, part):
    total = spectra.shape[1]
    window = NREC + LANES
    pair = BINS // freq_groups // 2
    lane = lax.broadcasted_iota(jnp.int32, (BINS // 2, LANES), 1)

    def one_shot(k, begin):
        base = pl.multiple_of(jnp.minimum((begin // LANES) * LANES, total - window), LANES)
        piece = spectra[:, pl.ds(base, window)]
        for first in range(0, slabs * HALF, 2 * LANES):
            at = chunk * slabs * HALF + first
            inv = inverse[:, at : at + 2 * LANES]
            offset = jnp.bitwise_and(inv - starts[k], NREC - 1)
            valid = (inv >= 0) & (offset < counts[k])
            target = jnp.where(valid, offset + (begin - base), -1)
            line = lax.broadcasted_iota(jnp.int32, (window, 2 * LANES), 0)
            hot = jnp.where(line == target, 1.0, 0.0).astype(jnp.bfloat16)
            placed = jnp.dot(piece, hot, preferred_element_type=jnp.float32)
            for half in range(2):
                slab = (first + half * LANES) // HALF
                value = placed[:, half * LANES : (half + 1) * LANES]
                for c in range(2):
                    mine = value[c * BINS : (c + 1) * BINS]
                    split = mine.reshape(freq_groups, 2, pair, LANES)
                    low = split[:, 0].reshape(freq_groups * pair, LANES)
                    high = split[:, 1].reshape(freq_groups * pair, LANES)
                    spot = pl.ds(c * shots + k, freq_groups * pair, stride=2 * shots)
                    part[slab, spot, :] = jnp.where(lane < HALF, low, pltpu.roll(high, HALF, 1))
                    part[slab + 1, spot, :] = jnp.where(lane < HALF, pltpu.roll(low, HALF, 1), high)
        return begin + counts[k]

    lax.fori_loop(0, shots, one_shot, 0, unroll=True)
    rows = pair * 2 * shots

    def deliver(group, carry):
        for slab in range(slabs):
            out[group * slabs + slab, segment * rows : (segment + 1) * rows, :] = part[
                slab, pl.ds(pl.multiple_of(group * rows, rows), rows), :
            ].astype(jnp.bfloat16)
        return carry

    lax.fori_loop(0, freq_groups, deliver, 0)


def stage_kernel(
    slabs, freq_groups, shots, row_steps, fresh, parts, with_positions,
    starts, counts, positions, inverse, *refs,
):
    refs = list(refs)
    part = refs.pop()
    step = pl.program_id(0)
    spectra = {}
    if fresh is not None:
        table, traces = refs[:2]
        mine, out = refs[-2:]
        known = refs[2:-2]
        spectra[fresh] = mine
        rows = traces.shape[0]
        block = jnp.dot(traces[...], table[...], preferred_element_type=jnp.float32)
        mine[:, pl.ds(pl.multiple_of(step * rows, rows), rows)] = block.astype(jnp.bfloat16).T
    else:
        out = refs[-1]
        known = refs[:-1]
    for half, ref in zip(sorted({h for h, _ in parts} - {fresh}), known):
        spectra[half] = ref

    @pl.when(step == row_steps - 1)
    def _place():
        for segment, (half, chunk) in enumerate(parts):
            place(
                slabs, freq_groups, shots, chunk, segment,
                starts, counts, inverse, spectra[half], out, part,
            )
        if not with_positions:
            return
        line = lax.broadcasted_iota(jnp.int32, (2 * shots, LANES), 0)
        halves = jnp.zeros((2 * shots, LANES), jnp.int32)
        for k in range(shots):
            halves = jnp.where(line == k, positions[k] // HALF, halves)
            halves = jnp.where(line == shots + k, positions[k] % HALF, halves)
        coded = halves.astype(jnp.float32).astype(jnp.bfloat16)
        rows_used = out.shape[1] - 2 * shots
        for dest in range(out.shape[0]):
            out[dest, rows_used:, :] = coded


def stage(
    traces, counts, starts, positions, inverse, slabs, freq_groups,
    fresh, parts, spectra, with_positions,
):
    row_total, samples = traces.shape
    shots = counts.shape[0]
    rows = 512
    row_steps = row_total // rows if fresh is not None else 1
    dests = freq_groups * slabs
    dest_rows = BINS // freq_groups // 2 * 2 * shots * len(parts)
    dest_rows += 2 * shots if with_positions else 0
    smem = pl.BlockSpec(memory_space=pltpu.SMEM)
    whole = pl.BlockSpec((2 * BINS, row_total), lambda i: (0, 0))
    shape = jax.ShapeDtypeStruct((2 * BINS, row_total), jnp.bfloat16)
    in_specs = [smem, smem, smem, pl.BlockSpec(inverse.shape, lambda i: (0, 0))]
    operands = [starts, counts, positions, inverse]
    out_specs = [pl.BlockSpec((dests, dest_rows, LANES), lambda i: (0, 0, 0))]
    out_shape = [jax.ShapeDtypeStruct((dests, dest_rows, LANES), jnp.bfloat16)]
    flops = len(parts) * 2 * 2 * BINS * shots * (NREC + LANES) * slabs * HALF
    if fresh is not None:
        in_specs += [
            pl.BlockSpec((samples, 2 * BINS), lambda i: (0, 0)),
            pl.BlockSpec((rows, samples), lambda i: (i, 0)),
        ]
        operands += [jnp.asarray(dft_table(samples, freq_groups, fresh)), traces]
        out_specs = [whole] + out_specs
        out_shape = [shape] + out_shape
        flops += 2 * row_total * samples * 2 * BINS
    for half in sorted({h for h, _ in parts} - {fresh}):
        in_specs.append(whole)
        operands.append(spectra[half])
    result = pl.pallas_call(
        functools.partial(
            stage_kernel, slabs, freq_groups, shots, row_steps, fresh, parts, with_positions
        ),
        grid=(row_steps,),
        in_specs=in_specs,
        out_specs=out_specs,
        out_shape=out_shape,
        scratch_shapes=[pltpu.VMEM((slabs, BINS * shots, LANES), jnp.float32)],
        compiler_params=pltpu.CompilerParams(vmem_limit_bytes=VMEM_BYTES),
        cost_estimate=pl.CostEstimate(
            flops=flops, bytes_accessed=row_total * samples * 2, transcendentals=0
        ),
        name="stage",
    )(*operands)
    if fresh is not None:
        spectra[fresh] = result[0]
    return result[-1]


def inverse_table(rec_slot, slabs, cap, chunks):
    slots = np.concatenate([chunk_columns(slabs, cap, chunk) for chunk in range(chunks)])
    receivers = jnp.arange(NREC, dtype=jnp.int32)
    return jnp.max(
        jnp.where(rec_slot[:, None] == jnp.asarray(slots)[None, :], receivers[:, None], -1), axis=0
    )[None, :]


def cos_sin(q, period):
    quarter = period // 4
    shifted = q + quarter // 2
    quadrant = jnp.bitwise_and(shifted // quarter, 3)
    x = (jnp.bitwise_and(shifted, quarter - 1) - quarter // 2).astype(jnp.float32) * (
        2.0 * math.pi / period
    )
    x2 = x * x
    sine = x + x * x2 * (
        -1.6666666666e-1 + x2 * (8.3333333e-3 + x2 * (-1.98412698e-4 + x2 * 2.7557319e-6))
    )
    cosine = 1.0 + x2 * (
        -0.5 + x2 * (4.16666667e-2 + x2 * (-1.38888889e-3 + x2 * 2.48015873e-5))
    )
    swap = jnp.bitwise_and(quadrant, 1) == 1
    c = jnp.where(swap, sine, cosine)
    s = jnp.where(swap, cosine, sine)
    c = jnp.where((quadrant == 1) | (quadrant == 2), -c, c)
    s = jnp.where(quadrant >= 2, -s, s)
    return c, s


def phase_kernel(shots, total_shots, pair, first_bin, halves, out):
    sources = halves.shape[0]
    coded = halves[...].reshape(sources, 2 * shots, LANES).astype(jnp.float32)
    positions = (coded[:, :shots] * HALF + coded[:, shots:]).astype(jnp.int32)
    rays = lax.broadcasted_iota(jnp.int32, positions.shape, 2) - RAY_PARAM_COUNT // 2
    period = NT * RDIV
    factor = 1.0 / math.sqrt(total_shots)
    for side in range(2):
        bin_index = first_bin[0] + pl.program_id(0) + side * pair
        q = jnp.bitwise_and(bin_index * rays * positions, period - 1)
        c, s = cos_sin(q, period)
        c = (c * factor)[:, None]
        s = (s * factor)[:, None]
        left = jnp.concatenate([c, s], axis=1).reshape(sources * 2 * shots, RAY_PARAM_COUNT)
        right = jnp.concatenate([-s, c], axis=1).reshape(sources * 2 * shots, RAY_PARAM_COUNT)
        at = 2 * side * RAY_PARAM_COUNT
        out[0, :, at : at + RAY_PARAM_COUNT] = left.astype(jnp.bfloat16)
        out[0, :, at + RAY_PARAM_COUNT : at + 2 * RAY_PARAM_COUNT] = right.astype(jnp.bfloat16)


def make_phases(received, first_bin, pair, shots):
    sources = received.shape[0]
    total_shots = sources * shots
    held = received.reshape(sources, -1, 2 * shots, LANES)
    last = held.shape[1] - 1
    return pl.pallas_call(
        functools.partial(phase_kernel, shots, total_shots, pair),
        grid=(pair,),
        in_specs=[
            pl.BlockSpec(memory_space=pltpu.SMEM),
            pl.BlockSpec((sources, 1, 2 * shots, LANES), lambda i: (0, last, 0, 0)),
        ],
        out_specs=pl.BlockSpec((1, 2 * total_shots, 4 * RAY_PARAM_COUNT), lambda i: (i, 0, 0)),
        out_shape=jax.ShapeDtypeStruct(
            (pair, 2 * total_shots, 4 * RAY_PARAM_COUNT), jnp.bfloat16
        ),
        compiler_params=pltpu.CompilerParams(vmem_limit_bytes=VMEM_BYTES),
        cost_estimate=pl.CostEstimate(
            flops=pair * total_shots * RAY_PARAM_COUNT * 80,
            bytes_accessed=32 * 1024 * 1024,
            transcendentals=0,
        ),
        name="phases",
    )(first_bin, held)


def encode_kernel(slots, pair, each, *refs):
    held, phases = refs[:2]
    out, summed = refs[-2:]
    step = pl.program_id(0)
    share = 2 * pair
    depth = phases.shape[1]
    width = 2 * RAY_PARAM_COUNT
    for item in range(each):
        value = lax.dot_general(
            held[:, item].reshape(depth, LANES),
            phases[item],
            (((0,), (0,)), ((), ())),
            preferred_element_type=jnp.float32,
        )
        for side in range(2):
            spot = pl.ds(step * each + item + side * pair, slots, stride=share)
            mine = value[side * HALF : side * HALF + slots, side * width : (side + 1) * width]
            for part in range(2):
                summed[part, spot, :] = mine[:, part * LANES : (part + 1) * LANES]

    @pl.when(step == pair // each - 1)
    def _round():
        for part in range(2):
            out[:, :, part * LANES : (part + 1) * LANES] = (
                summed[part].reshape(slots, share, LANES).astype(jnp.bfloat16)
            )


def encode(received, phases, before, segment, chunk, half, cap, freq_block, shots):
    sources = received.shape[0]
    share = freq_block // HALVES
    pair = share // 2
    each = 2
    group = 2 * shots
    held = received.reshape(sources, -1, group, LANES)
    slots = min(cap, HALF)
    depth = phases.shape[1]
    in_specs = [
        pl.BlockSpec(
            (sources, each, group, LANES), lambda i: (0, segment * (pair // each) + i, 0, 0)
        ),
        pl.BlockSpec((each, depth, 4 * RAY_PARAM_COUNT), lambda i: (i, 0, 0)),
    ]
    operands = [held, phases]
    aliases = {}
    if before is not None:
        in_specs.append(pl.BlockSpec(memory_space=pl.ANY))
        operands.append(before)
        aliases = {2: 0}
    return pl.pallas_call(
        functools.partial(encode_kernel, slots, pair, each),
        grid=(pair // each,),
        in_specs=in_specs,
        out_specs=pl.BlockSpec((slots, share, 2 * RAY_PARAM_COUNT), lambda i: (chunk, half, 0)),
        out_shape=jax.ShapeDtypeStruct((cap, freq_block, 2 * RAY_PARAM_COUNT), jnp.bfloat16),
        scratch_shapes=[pltpu.VMEM((2, slots * share, LANES), jnp.float32)],
        input_output_aliases=aliases,
        compiler_params=pltpu.CompilerParams(vmem_limit_bytes=VMEM_BYTES),
        cost_estimate=pl.CostEstimate(
            flops=2 * share * depth * LANES * 2 * RAY_PARAM_COUNT,
            bytes_accessed=16 * 1024 * 1024,
            transcendentals=0,
        ),
        name="encode",
    )(*operands)


def on_device(traces, trace_counts, aperture_start, shot_position, rec_slot):
    shots = trace_counts.shape[1]
    freq_groups = lax.axis_size("freq")
    slabs = lax.axis_size("slab")
    freq_block = FREQUENCY_COUNT // freq_groups
    share = freq_block // HALVES
    cap = 3 * NREC // (2 * slabs)
    chunks = -(-cap // HALF)
    assert cap % min(cap, HALF) == 0
    counts = trace_counts[0]
    inverse = inverse_table(rec_slot, slabs, cap, chunks)
    own_bin = F0 + lax.axis_index("freq") * freq_block
    first_bins = [(own_bin + half * share).astype(jnp.int32)[None] for half in range(HALVES)]
    order = [(half, chunk) for half in range(HALVES) for chunk in range(chunks)]
    groups = [order[:1], order[1:-1], order[-1:]]
    groups = [group for group in groups if group]
    spectra = {}

    def make(index):
        missing = [h for h, _ in groups[index] if h not in spectra]
        return stage(
            traces, counts, aperture_start, shot_position, inverse, slabs, freq_groups,
            missing[0] if missing else None, groups[index], spectra, index == 0,
        )

    phases, encoded = None, None
    received = exchange(make(0))
    for index, group in enumerate(groups):
        upcoming = None
        if index == 0 and len(groups) > 2:
            upcoming = exchange(make(1))
        elif index + 1 < len(groups):
            tied = lax.optimization_barrier((received, make(index + 1), phases, encoded))
            received, sent, phases, encoded = tied
            upcoming = exchange(sent)
        if index == 0:
            phases = [make_phases(received, first, share // 2, shots) for first in first_bins]
        for segment, (half, chunk) in enumerate(group):
            encoded = encode(
                received, phases[half], encoded, segment, chunk, half, cap, freq_block, shots
            )
        received = upcoming
    return encoded


def exchange(sent):
    return lax.all_to_all(sent, ("freq", "slab"), split_axis=0, concat_axis=0, tiled=True)


def solution(mesh):
    return jax.shard_map(
        on_device,
        mesh=mesh,
        in_specs=(
            P(("freq", "slab"), None),
            P(("freq", "slab"), None),
            P(("freq", "slab")),
            P(("freq", "slab")),
            P(),
        ),
        out_specs=P("slab", "freq", None),
        check_vma=False,
    )
```

```python
import functools
import math

import jax
import jax.numpy as jnp
import ml_dtypes
import numpy as np
from jax import lax
from jax.experimental import pallas as pl
from jax.experimental.pallas import tpu as pltpu
from jax.sharding import PartitionSpec as P

NT = 2048
FREQUENCY_COUNT = 256
F0 = 8
RAY_PARAM_COUNT = 128
NREC = 512
RDIV = 16
LANES = 128
HALF = 64
HALVES = 2
BINS = FREQUENCY_COUNT // HALVES
VMEM_BYTES = 63 * 1024 * 1024


def dft_table(samples, freq_groups, half):
    share = FREQUENCY_COUNT // freq_groups // HALVES
    owners = np.arange(freq_groups, dtype=np.int64)[:, None] * (HALVES * share)
    bins = (F0 + owners + half * share + np.arange(share, dtype=np.int64)[None, :]).reshape(-1)
    index = (np.arange(samples, dtype=np.int64)[:, None] * bins[None, :]) % samples
    angle = index.astype(np.float64) * (2.0 * math.pi / samples)
    factor = 1.0 / math.sqrt(samples)
    table = np.concatenate([np.cos(angle), -np.sin(angle)], axis=1) * factor
    return table.astype(np.float32).astype(ml_dtypes.bfloat16)


def chunk_columns(slabs, cap, chunk):
    lane = chunk * HALF + np.arange(HALF)
    slots = [np.where(lane < cap, slab * cap + lane, -2) for slab in range(slabs)]
    return np.concatenate(slots).astype(np.int32)


def place(slabs, freq_groups, shots, chunk, segment, starts, counts, inverse, spectra, out, part):
    total = spectra.shape[1]
    window = NREC + LANES
    pair = BINS // freq_groups // 2
    lane = lax.broadcasted_iota(jnp.int32, (BINS // 2, LANES), 1)

    def one_shot(k, begin):
        base = pl.multiple_of(jnp.minimum((begin // LANES) * LANES, total - window), LANES)
        piece = spectra[:, pl.ds(base, window)]
        for first in range(0, slabs * HALF, 2 * LANES):
            at = chunk * slabs * HALF + first
            inv = inverse[:, at : at + 2 * LANES]
            offset = jnp.bitwise_and(inv - starts[k], NREC - 1)
            valid = (inv >= 0) & (offset < counts[k])
            target = jnp.where(valid, offset + (begin - base), -1)
            line = lax.broadcasted_iota(jnp.int32, (window, 2 * LANES), 0)
            hot = jnp.where(line == target, 1.0, 0.0).astype(jnp.bfloat16)
            placed = jnp.dot(piece, hot, preferred_element_type=jnp.float32)
            for half in range(2):
                slab = (first + half * LANES) // HALF
                value = placed[:, half * LANES : (half + 1) * LANES]
                for c in range(2):
                    mine = value[c * BINS : (c + 1) * BINS]
                    split = mine.reshape(freq_groups, 2, pair, LANES)
                    low = split[:, 0].reshape(freq_groups * pair, LANES)
                    high = split[:, 1].reshape(freq_groups * pair, LANES)
                    spot = pl.ds(c * shots + k, freq_groups * pair, stride=2 * shots)
                    part[slab, spot, :] = jnp.where(lane < HALF, low, pltpu.roll(high, HALF, 1))
                    part[slab + 1, spot, :] = jnp.where(lane < HALF, pltpu.roll(low, HALF, 1), high)
        return begin + counts[k]

    lax.fori_loop(0, shots, one_shot, 0, unroll=True)
    rows = pair * 2 * shots

    def deliver(group, carry):
        for slab in range(slabs):
            out[group * slabs + slab, segment * rows : (segment + 1) * rows, :] = part[
                slab, pl.ds(pl.multiple_of(group * rows, rows), rows), :
            ].astype(jnp.bfloat16)
        return carry

    lax.fori_loop(0, freq_groups, deliver, 0, unroll=True)


def stage_kernel(
    slabs, freq_groups, shots, row_steps, fresh, parts, with_positions,
    starts, counts, positions, inverse, *refs,
):
    refs = list(refs)
    part = refs.pop()
    step = pl.program_id(0)
    spectra = {}
    if fresh is not None:
        table, traces = refs[:2]
        mine, out = refs[-2:]
        known = refs[2:-2]
        spectra[fresh] = mine
        rows = traces.shape[0]
        block = jnp.dot(traces[...], table[...], preferred_element_type=jnp.float32)
        mine[:, pl.ds(pl.multiple_of(step * rows, rows), rows)] = block.astype(jnp.bfloat16).T
    else:
        out = refs[-1]
        known = refs[:-1]
    for half, ref in zip(sorted({h for h, _ in parts} - {fresh}), known):
        spectra[half] = ref

    @pl.when(step == row_steps - 1)
    def _place():
        for segment, (half, chunk) in enumerate(parts):
            place(
                slabs, freq_groups, shots, chunk, segment,
                starts, counts, inverse, spectra[half], out, part,
            )
        if not with_positions:
            return
        line = lax.broadcasted_iota(jnp.int32, (2 * shots, LANES), 0)
        halves = jnp.zeros((2 * shots, LANES), jnp.int32)
        for k in range(shots):
            halves = jnp.where(line == k, positions[k] // HALF, halves)
            halves = jnp.where(line == shots + k, positions[k] % HALF, halves)
        coded = halves.astype(jnp.float32).astype(jnp.bfloat16)
        rows_used = out.shape[1] - 2 * shots
        for dest in range(out.shape[0]):
            out[dest, rows_used:, :] = coded


def stage(
    traces, counts, starts, positions, inverse, slabs, freq_groups,
    fresh, parts, spectra, with_positions,
):
    row_total, samples = traces.shape
    shots = counts.shape[0]
    rows = 512
    row_steps = row_total // rows if fresh is not None else 1
    dests = freq_groups * slabs
    dest_rows = BINS // freq_groups // 2 * 2 * shots * len(parts)
    dest_rows += 2 * shots if with_positions else 0
    smem = pl.BlockSpec(memory_space=pltpu.SMEM)
    whole = pl.BlockSpec((2 * BINS, row_total), lambda i: (0, 0))
    shape = jax.ShapeDtypeStruct((2 * BINS, row_total), jnp.bfloat16)
    in_specs = [smem, smem, smem, pl.BlockSpec(inverse.shape, lambda i: (0, 0))]
    operands = [starts, counts, positions, inverse]
    out_specs = [pl.BlockSpec((dests, dest_rows, LANES), lambda i: (0, 0, 0))]
    out_shape = [jax.ShapeDtypeStruct((dests, dest_rows, LANES), jnp.bfloat16)]
    flops = len(parts) * 2 * 2 * BINS * shots * (NREC + LANES) * slabs * HALF
    if fresh is not None:
        in_specs += [
            pl.BlockSpec((samples, 2 * BINS), lambda i: (0, 0)),
            pl.BlockSpec((rows, samples), lambda i: (i, 0)),
        ]
        operands += [jnp.asarray(dft_table(samples, freq_groups, fresh)), traces]
        out_specs = [whole] + out_specs
        out_shape = [shape] + out_shape
        flops += 2 * row_total * samples * 2 * BINS
    for half in sorted({h for h, _ in parts} - {fresh}):
        in_specs.append(whole)
        operands.append(spectra[half])
    result = pl.pallas_call(
        functools.partial(
            stage_kernel, slabs, freq_groups, shots, row_steps, fresh, parts, with_positions
        ),
        grid=(row_steps,),
        in_specs=in_specs,
        out_specs=out_specs,
        out_shape=out_shape,
        scratch_shapes=[pltpu.VMEM((slabs, BINS * shots, LANES), jnp.float32)],
        compiler_params=pltpu.CompilerParams(vmem_limit_bytes=VMEM_BYTES),
        cost_estimate=pl.CostEstimate(
            flops=flops, bytes_accessed=row_total * samples * 2, transcendentals=0
        ),
        name="stage",
    )(*operands)
    if fresh is not None:
        spectra[fresh] = result[0]
    return result[-1]


def inverse_table(rec_slot, slabs, cap, chunks):
    slots = np.concatenate([chunk_columns(slabs, cap, chunk) for chunk in range(chunks)])
    receivers = jnp.arange(NREC, dtype=jnp.int32)
    return jnp.max(
        jnp.where(rec_slot[:, None] == jnp.asarray(slots)[None, :], receivers[:, None], -1), axis=0
    )[None, :]


def cos_sin(q, period):
    quarter = period // 4
    shifted = q + quarter // 2
    quadrant = jnp.bitwise_and(shifted // quarter, 3)
    x = (jnp.bitwise_and(shifted, quarter - 1) - quarter // 2).astype(jnp.float32) * (
        2.0 * math.pi / period
    )
    x2 = x * x
    sine = x + x * x2 * (
        -1.6666666666e-1 + x2 * (8.3333333e-3 + x2 * (-1.98412698e-4 + x2 * 2.7557319e-6))
    )
    cosine = 1.0 + x2 * (
        -0.5 + x2 * (4.16666667e-2 + x2 * (-1.38888889e-3 + x2 * 2.48015873e-5))
    )
    swap = jnp.bitwise_and(quadrant, 1) == 1
    c = jnp.where(swap, sine, cosine)
    s = jnp.where(swap, cosine, sine)
    c = jnp.where((quadrant == 1) | (quadrant == 2), -c, c)
    s = jnp.where(quadrant >= 2, -s, s)
    return c, s


def phase_kernel(shots, total_shots, pair, first_bin, halves, out):
    sources = halves.shape[0]
    coded = halves[...].reshape(sources, 2 * shots, LANES).astype(jnp.float32)
    positions = (coded[:, :shots] * HALF + coded[:, shots:]).astype(jnp.int32)
    rays = lax.broadcasted_iota(jnp.int32, positions.shape, 2) - RAY_PARAM_COUNT // 2
    period = NT * RDIV
    factor = 1.0 / math.sqrt(total_shots)
    for side in range(2):
        bin_index = first_bin[0] + pl.program_id(0) + side * pair
        q = jnp.bitwise_and(bin_index * rays * positions, period - 1)
        c, s = cos_sin(q, period)
        c = (c * factor)[:, None]
        s = (s * factor)[:, None]
        left = jnp.concatenate([c, s], axis=1).reshape(sources * 2 * shots, RAY_PARAM_COUNT)
        right = jnp.concatenate([-s, c], axis=1).reshape(sources * 2 * shots, RAY_PARAM_COUNT)
        at = 2 * side * RAY_PARAM_COUNT
        out[0, :, at : at + RAY_PARAM_COUNT] = left.astype(jnp.bfloat16)
        out[0, :, at + RAY_PARAM_COUNT : at + 2 * RAY_PARAM_COUNT] = right.astype(jnp.bfloat16)


def make_phases(received, first_bin, pair, shots):
    sources = received.shape[0]
    total_shots = sources * shots
    held = received.reshape(sources, -1, 2 * shots, LANES)
    last = held.shape[1] - 1
    return pl.pallas_call(
        functools.partial(phase_kernel, shots, total_shots, pair),
        grid=(pair,),
        in_specs=[
            pl.BlockSpec(memory_space=pltpu.SMEM),
            pl.BlockSpec((sources, 1, 2 * shots, LANES), lambda i: (0, last, 0, 0)),
        ],
        out_specs=pl.BlockSpec((1, 2 * total_shots, 4 * RAY_PARAM_COUNT), lambda i: (i, 0, 0)),
        out_shape=jax.ShapeDtypeStruct(
            (pair, 2 * total_shots, 4 * RAY_PARAM_COUNT), jnp.bfloat16
        ),
        compiler_params=pltpu.CompilerParams(vmem_limit_bytes=VMEM_BYTES),
        cost_estimate=pl.CostEstimate(
            flops=pair * total_shots * RAY_PARAM_COUNT * 80,
            bytes_accessed=32 * 1024 * 1024,
            transcendentals=0,
        ),
        name="phases",
    )(first_bin, held)


def encode_kernel(slots, pair, each, *refs):
    held, phases = refs[:2]
    out, summed = refs[-2:]
    step = pl.program_id(0)
    share = 2 * pair
    depth = phases.shape[1]
    width = 2 * RAY_PARAM_COUNT
    for item in range(each):
        value = lax.dot_general(
            held[:, item].reshape(depth, LANES),
            phases[item],
            (((0,), (0,)), ((), ())),
            preferred_element_type=jnp.float32,
        )
        for side in range(2):
            spot = pl.ds(step * each + item + side * pair, slots, stride=share)
            mine = value[side * HALF : side * HALF + slots, side * width : (side + 1) * width]
            for part in range(2):
                summed[part, spot, :] = mine[:, part * LANES : (part + 1) * LANES]

    @pl.when(step == pair // each - 1)
    def _round():
        for part in range(2):
            out[:, :, part * LANES : (part + 1) * LANES] = (
                summed[part].reshape(slots, share, LANES).astype(jnp.bfloat16)
            )


def encode(received, phases, before, segment, chunk, half, cap, freq_block, shots):
    sources = received.shape[0]
    share = freq_block // HALVES
    pair = share // 2
    each = 2
    group = 2 * shots
    held = received.reshape(sources, -1, group, LANES)
    slots = min(cap, HALF)
    depth = phases.shape[1]
    in_specs = [
        pl.BlockSpec(
            (sources, each, group, LANES), lambda i: (0, segment * (pair // each) + i, 0, 0)
        ),
        pl.BlockSpec((each, depth, 4 * RAY_PARAM_COUNT), lambda i: (i, 0, 0)),
    ]
    operands = [held, phases]
    aliases = {}
    if before is not None:
        in_specs.append(pl.BlockSpec(memory_space=pl.ANY))
        operands.append(before)
        aliases = {2: 0}
    return pl.pallas_call(
        functools.partial(encode_kernel, slots, pair, each),
        grid=(pair // each,),
        in_specs=in_specs,
        out_specs=pl.BlockSpec((slots, share, 2 * RAY_PARAM_COUNT), lambda i: (chunk, half, 0)),
        out_shape=jax.ShapeDtypeStruct((cap, freq_block, 2 * RAY_PARAM_COUNT), jnp.bfloat16),
        scratch_shapes=[pltpu.VMEM((2, slots * share, LANES), jnp.float32)],
        input_output_aliases=aliases,
        compiler_params=pltpu.CompilerParams(vmem_limit_bytes=VMEM_BYTES),
        cost_estimate=pl.CostEstimate(
            flops=2 * share * depth * LANES * 2 * RAY_PARAM_COUNT,
            bytes_accessed=16 * 1024 * 1024,
            transcendentals=0,
        ),
        name="encode",
    )(*operands)


def on_device(traces, trace_counts, aperture_start, shot_position, rec_slot):
    shots = trace_counts.shape[1]
    freq_groups = lax.axis_size("freq")
    slabs = lax.axis_size("slab")
    freq_block = FREQUENCY_COUNT // freq_groups
    share = freq_block // HALVES
    cap = 3 * NREC // (2 * slabs)
    chunks = -(-cap // HALF)
    assert cap % min(cap, HALF) == 0
    counts = trace_counts[0]
    inverse = inverse_table(rec_slot, slabs, cap, chunks)
    own_bin = F0 + lax.axis_index("freq") * freq_block
    first_bins = [(own_bin + half * share).astype(jnp.int32)[None] for half in range(HALVES)]
    order = [(half, chunk) for half in range(HALVES) for chunk in range(chunks)]
    groups = [order[:1], order[1:-1], order[-1:]]
    groups = [group for group in groups if group]
    spectra = {}

    def make(index):
        missing = [h for h, _ in groups[index] if h not in spectra]
        return stage(
            traces, counts, aperture_start, shot_position, inverse, slabs, freq_groups,
            missing[0] if missing else None, groups[index], spectra, index == 0,
        )

    phases, encoded = None, None
    received = exchange(make(0))
    for index, group in enumerate(groups):
        upcoming = None
        if index + 1 < len(groups):
            tied = lax.optimization_barrier((received, make(index + 1), phases, encoded))
            received, sent, phases, encoded = tied
            upcoming = exchange(sent)
        if index == 0:
            phases = [make_phases(received, first, share // 2, shots) for first in first_bins]
        for segment, (half, chunk) in enumerate(group):
            encoded = encode(
                received, phases[half], encoded, segment, chunk, half, cap, freq_block, shots
            )
        received = upcoming
    return encoded


def exchange(sent):
    return lax.all_to_all(sent, ("freq", "slab"), split_axis=0, concat_axis=0, tiled=True)


def solution(mesh):
    return jax.shard_map(
        on_device,
        mesh=mesh,
        in_specs=(
            P(("freq", "slab"), None),
            P(("freq", "slab"), None),
            P(("freq", "slab")),
            P(("freq", "slab")),
            P(),
        ),
        out_specs=P("slab", "freq", None),
        check_vma=False,
    )
```
